32 devices in a mesh: row: 8 (over z, core), col: 4 (over y, x).
Axes of the slice: x: 2, y: 2, z: 4, core: 2. Of those that a mesh axis runs over, the one named last changes fastest.
Arguments:
- inputs: bfloat16 [3, 64, 64, 512], P(None, None, 'row', 'col'), may hold values from -6 to 6
- gate_pre: bfloat16 [3, 256, 64, 512], P(None, None, 'row', 'col'), may hold values from -8 to 8
- cotangent: bfloat16 [3, 64, 64, 512], P(None, None, 'row', 'col'), may hold values from -6 to 6
- hidden_init: bfloat16 [64, 64, 512], P(None, 'row', 'col'), may hold values from -6 to 6
- cell_init: float32 [64, 64, 512], P(None, 'row', 'col'), may hold values from -6 to 6
- land_mask: int32 [64, 512], P('row', 'col'), may hold values 0 or 1
- kernel: bfloat16 [256, 1152], replicated, may hold values from -0.1875 to 0.1875
Outputs:
- grad_inputs: bfloat16 [3, 64, 64, 512], P(None, None, 'row', 'col')
- grad_hidden: float32 [64, 64, 512], P(None, 'row', 'col')
- grad_cell: float32 [64, 64, 512], P(None, 'row', 'col')
- grad_kernel: float32 [256, 1152], P('row', 'col')
- grad_bias: float32 [256], P(('row', 'col'))
The draws below stay inside these ranges and needn't reach their ends.
Inputs may be any that keep to these rules, and one draw needn't show every extreme that they name: `land_mask`: 1 marks a land cell.
All inputs are finite; a program needn't handle non-finite values. No bound on the sum of `land_mask` on one device may be relied on, other than what follows from the above.
Results may differ from the reference program's by a relative error of at most 0.005.
Values may be sent and summed in bfloat16 or wider, within the bound.
A program may use at most 64 MiB of HBM per device.

```python
import jax
import jax.numpy as jnp
from jax import lax

IN = 64
HID = 64
STEPS = 3
NH = 64
NW = 512
GATES = 256
TAPS = 1152


def place_ends(result, own_key, smallest, largest):
    index_at = [jax.random.randint(jax.random.fold_in(own_key, axis), (), 0, length) for axis, length in enumerate(result.shape)]
    main_axis = result.shape.index(max(result.shape))
    beside = index_at[:main_axis] + [(index_at[main_axis] + 1) % result.shape[main_axis]] + index_at[main_axis + 1:]
    return result.at[tuple(index_at)].set(smallest).at[tuple(beside)].set(largest)


def block_scale(key, shape, pieces, low, top_value):
    gain = 1.0
    for position, shards_of in pieces:
        steps = jax.random.uniform(jax.random.fold_in(jax.random.fold_in(key, 6), position), (shards_of,), jnp.float32, low / len(pieces), top_value / len(pieces))
        gain = gain * jnp.repeat(jnp.exp(steps), shape[position] // shards_of).reshape((-1,) + (1,) * (len(shape) - 1 - position))
    return gain


def scatter_about(stream_key, shape, spread, bound, split=(), dtype=jnp.bfloat16):
    values = jax.random.normal(stream_key, shape, jnp.float32) * spread
    if len(split) > 0:
        values = block_scale(stream_key, shape, split, -0.22, 0.18) * values
    return jnp.clip(values, min=-bound, max=bound).astype(dtype)


def setup_inputs(seed: int = 0) -> dict:
    arg_keys = jax.random.split(jax.random.key(seed), 8)
    inputs = scatter_about(arg_keys[0], (STEPS, IN, NH, NW), 1.0, 6.0, ((2, 8), (3, 4)))
    gate_pre = scatter_about(arg_keys[1], (STEPS, GATES, NH, NW), 1.5, 8.0, ((2, 8), (3, 4)))
    cotangent = scatter_about(arg_keys[2], (STEPS, HID, NH, NW), 1.0, 6.0, ((2, 8), (3, 4)))
    hidden_init = scatter_about(arg_keys[3], (HID, NH, NW), 1.0, 6.0, ((1, 8), (2, 4)))
    cell_init = scatter_about(arg_keys[4], (HID, NH, NW), 1.0, 6.0, ((1, 8), (2, 4)), jnp.float32)
    land_mask = place_ends((jax.random.randint(arg_keys[5], (NH, NW), 0, 4) < 3).astype(jnp.int32), jax.random.fold_in(arg_keys[5], 1), 0, 1)
    kernel = scatter_about(arg_keys[6], (GATES, TAPS), TAPS ** -0.5, 0.1875)
    return {"inputs": inputs, "gate_pre": gate_pre, "cotangent": cotangent, "hidden_init": hidden_init, "cell_init": cell_init, "land_mask": land_mask, "kernel": kernel}


def gate_parts(pre, hidden):
    return (jax.nn.sigmoid(pre[:hidden]), jax.nn.sigmoid(pre[hidden:2 * hidden]), jax.nn.sigmoid(pre[2 * hidden:3 * hidden]), jnp.tanh(pre[3 * hidden:]))

def kernel_terms(grads, padded, rows, cols):
    flat = grads.reshape(grads.shape[0], rows * cols)
    blocks = []
    for offset in range(9):
        upper, left = (offset // 3, offset % 3)
        window = padded[:, upper:upper + rows, left:left + cols].reshape(padded.shape[0], rows * cols)
        blocks.append(lax.dot_general(flat, window, (((1,), (1,)), ((), ())), preferred_element_type=jnp.float32))
    return jnp.concatenate(blocks, axis=1)

def transposed(kernel, padded_grads, rows, cols, width):
    total = jnp.zeros((width, rows * cols), jnp.float32)
    for offset in range(9):
        upper, left = (offset // 3, offset % 3)
        window = padded_grads[:, 2 - upper:2 - upper + rows, 2 - left:2 - left + cols]
        window = window.reshape(padded_grads.shape[0], rows * cols)
        piece = kernel[:, offset * width:(offset + 1) * width]
        total = total + lax.dot_general(piece, window, (((0,), (0,)), ((), ())), preferred_element_type=jnp.float32)
    return total

def reference(inputs, gate_pre, cotangent, hidden_init, cell_init, land_mask, kernel):
    mask = land_mask.astype(jnp.float32)
    scale = 1.0 / jnp.sqrt(jnp.float32(NH * NW))
    width = IN + HID
    states = [cell_init]
    layers = []
    hidden_now = hidden_init
    acts = []
    for step in range(STEPS):
        gates = gate_parts(gate_pre[step].astype(jnp.float32), HID)
        acts.append(gates)
        layers.append(jnp.concatenate([inputs[step], hidden_now], axis=0))
        new_cell = gates[1] * states[-1] + gates[0] * gates[3]
        states.append(new_cell)
        hidden_now = (mask * gates[2] * jnp.tanh(new_cell)).astype(jnp.bfloat16)
    grad_h = jnp.zeros((HID, NH, NW), jnp.float32)
    grad_c = jnp.zeros((HID, NH, NW), jnp.float32)
    kernel_total = jnp.zeros((4 * HID, 9 * width), jnp.float32)
    bias_total = jnp.zeros((4 * HID,), jnp.float32)
    outs = [None] * STEPS
    for step in reversed(range(STEPS)):
        gin, gfor, gout, gcand = acts[step]
        tanh_cell = jnp.tanh(states[step + 1])
        error = mask * (grad_h + cotangent[step].astype(jnp.float32))
        grad_c = grad_c + error * gout * (1.0 - tanh_cell * tanh_cell)
        grads = jnp.concatenate([grad_c * gcand * gin * (1.0 - gin), grad_c * states[step] * gfor * (1.0 - gfor), error * tanh_cell * gout * (1.0 - gout), grad_c * gin * (1.0 - gcand * gcand)], axis=0).astype(jnp.bfloat16)
        grad_c = grad_c * gfor
        padded = jnp.pad(layers[step], ((0, 0), (1, 1), (1, 1)))
        kernel_total = kernel_total + scale * kernel_terms(grads, padded, NH, NW)
        bias_total = bias_total + scale * lax.optimization_barrier(jnp.sum(grads.astype(jnp.float32), axis=(1, 2)))
        padded_grads = jnp.pad(grads, ((0, 0), (1, 1), (1, 1)))
        back = transposed(kernel, padded_grads, NH, NW, width)
        outs[step] = back[:IN].reshape(IN, NH, NW).astype(jnp.bfloat16)
        grad_h = back[IN:].reshape(HID, NH, NW)
    return (jnp.stack(outs), grad_h, grad_c, kernel_total, bias_total)
```

```python
import functools
import math

import jax
import jax.numpy as jnp
from jax import lax
from jax.experimental import pallas as pl
from jax.experimental.pallas import tpu as pltpu
from jax.sharding import PartitionSpec as P

MESH = pl.DeviceIdType.MESH
F32 = jnp.float32
BF16 = jnp.bfloat16
SIDES = ((-1, 0), (1, 0), (0, 1), (1, 1), (-1, 1), (0, -1), (1, -1), (-1, -1))
BLOCK = 16


def nt(lhs, rhs):
    return lax.dot_general(lhs, rhs, (((1,), (1,)), ((), ())), preferred_element_type=F32)


def nn(lhs, rhs):
    return jnp.dot(lhs, rhs, preferred_element_type=F32)


def sigmoid(value):
    return 0.5 * jnp.tanh(0.5 * value) + 0.5


def body(
    dims,
    inp_in, pre_in, cot_in, hid_in, cell_in, mask_in, weight_in,
    gin_hbm, gh_hbm, gc_hbm, gk_hbm, bias_hbm,
    inp, pre, cot, hid, cell, mask, weight, load_sem,
    acts, cells, tanhs, gradc, nat, zst, aall, edges, border, shifter, weight_t, selector,
    product, kacc, kfull, kown, kbuf, r1, s1own, s1, r2, s2own, s2, r3,
    send_sem, recv_sem, rs_send, rs_recv,
    gin_out, gh_out, gc_out, gk_out, bias_out, store_sem,
):
    steps, cin, hidden, rows, cols, nrow, ncol = dims
    width = cin + hidden
    gates = 4 * hidden
    padded = (rows + 2) * cols
    edge = edges.shape[2]
    half = nrow // 2
    high = gates // nrow
    part = weight.shape[1] // ncol
    lanes = kbuf.shape[-1]
    row, col = lax.axis_index("row"), lax.axis_index("col")
    zpos, core = row // 2, row % 2
    scale = 1.0 / math.sqrt(rows * cols * nrow * ncol)

    def inside(r, c):
        return (r >= 0) & (r < nrow) & (c >= 0) & (c < ncol)

    loads = [pltpu.make_async_copy(pre_in.at[step], pre.at[step], load_sem.at[step]) for step in range(steps)]
    for n, (source, target) in enumerate(
        ((cell_in, cell), (mask_in, mask), (weight_in, weight), (cot_in, cot), (inp_in, inp), (hid_in, hid))
    ):
        loads.append(pltpu.make_async_copy(source, target, load_sem.at[steps + n]))
    for n in (0, steps, steps + 1, steps + 2, *range(1, steps), steps + 3, steps + 4, steps + 5):
        loads[n].start()

    border[...] = jnp.zeros_like(border)
    for step in range(steps):
        aall[step, gates : 2 * gates, 0:cols] = jnp.zeros((gates, cols), BF16)
        aall[step, gates : 2 * gates, padded - cols : padded] = jnp.zeros((gates, cols), BF16)

    barrier = pltpu.get_barrier_semaphore()
    for dr, dc in SIDES:
        @pl.when(inside(row + dr, col + dc))
        def _():
            pl.semaphore_signal(barrier, inc=1, device_id=(row + dr, col + dc), device_id_type=MESH)
    sibling = row + 1 - 2 * core
    pl.semaphore_signal(barrier, inc=1, device_id=(sibling, col), device_id_type=MESH)
    for j in range(1, ncol):
        pl.semaphore_signal(barrier, inc=1, device_id=(row, (col + j) % ncol), device_id_type=MESH)
    for j in range(1, half):
        pl.semaphore_signal(barrier, inc=1, device_id=(((zpos + j) % half) * 2 + core, col), device_id_type=MESH)

    srow = lax.broadcasted_iota(jnp.int32, (2 * cols, 2 * cols), 0)
    scol = lax.broadcasted_iota(jnp.int32, (2 * cols, 2 * cols), 1)
    for j in range(rows + 2):
        if j == 0:
            low, up = edge + rows - 1, 4 * edge + rows - 1
        elif j == rows + 1:
            low, up = 2 * edge, 5 * edge
        else:
            low, up = j - 1, 3 * edge + j - 1
        source = jnp.where(
            scol < cols,
            jnp.where(scol == 0, cols + low, scol - 1),
            jnp.where(scol == 2 * cols - 1, cols + up, scol - cols + 1),
        )
        shifter[j] = (srow == source).astype(F32).astype(BF16)
    prow = lax.broadcasted_iota(jnp.int32, selector.shape, 0)
    pcol = lax.broadcasted_iota(jnp.int32, selector.shape, 1)
    wanted = jnp.where(prow < edge, prow * cols, (prow - edge) * cols + cols - 1)
    valid = (prow % edge) < rows
    selector[...] = ((pcol == wanted) & valid).astype(F32).astype(BF16)
    irow = lax.broadcasted_iota(jnp.int32, (gates, gates), 0)
    icol = lax.broadcasted_iota(jnp.int32, (gates, gates), 1)
    identity = (irow == icol).astype(F32).astype(BF16)

    loads[0].wait()
    loads[steps].wait()
    loads[steps + 1].wait()
    land = mask[...].astype(F32)[None]
    cells[0] = cell[...]
    gradc[...] = jnp.zeros_like(gradc)

    def place_z(step, first, count):
        for r in range(rows):
            tile = nat[pl.ds(r, count, stride=rows), :].astype(BF16)
            for dr in range(3):
                at = (r + 2 - dr) * cols
                zst[step, dr * width + first : dr * width + first + count, at : at + cols] = tile

    for step in range(steps):
        for dr in range(3):
            for i in range(rows + 2):
                if not 0 <= i + dr - 2 < rows:
                    zst[step, dr * width : (dr + 1) * width, i * cols : (i + 1) * cols] = jnp.zeros((width, cols), BF16)

    def spread(ref, step=None):
        def put(b, carry):
            at = pl.ds(b * BLOCK, BLOCK)
            value = (ref[at] if step is None else ref[step, at]).astype(F32)
            nat[pl.ds(b * BLOCK * rows, BLOCK * rows), :] = value.reshape(BLOCK * rows, cols)
            return carry
        lax.fori_loop(0, ref.shape[-3] // BLOCK, put, 0)

    for step in range(steps):
        if step:
            loads[step].wait()

        def forward(b, carry):
            def gate(n):
                return pre[step, pl.ds(n * hidden + b * BLOCK, BLOCK)].astype(F32)
            at = pl.ds(b * BLOCK, BLOCK)
            gi, gf, go, gg = sigmoid(gate(0)), sigmoid(gate(1)), sigmoid(gate(2)), jnp.tanh(gate(3))
            new = gf * cells[step, at] + gi * gg
            tn = jnp.tanh(new)
            acts[step, 0, at] = gi
            acts[step, 1, at] = gf
            acts[step, 2, at] = go
            acts[step, 3, at] = gg
            cells[step + 1, at] = new
            tanhs[step, at] = tn
            nat[pl.ds(b * BLOCK * rows, BLOCK * rows), :] = (land * go * tn).reshape(BLOCK * rows, cols)
            return carry
        lax.fori_loop(0, hidden // BLOCK, forward, 0)
        if step + 1 < steps:
            place_z(step + 1, cin, hidden)

    loads[steps + 3].wait()

    def halo(step, d):
        dr, dc = SIDES[d]
        if dc == 0:
            first = cols if dr < 0 else rows * cols
            land_at = padded - cols if dr < 0 else 0
            src = aall.at[step, pl.ds(gates, gates), pl.ds(first, cols)]
            dst = aall.at[step, pl.ds(gates, gates), pl.ds(land_at, cols)]
        else:
            src = edges.at[step, 1 if dc > 0 else 0]
            dst = border.at[step, pl.ds((d - 2) * edge, edge)]
        return pltpu.make_async_remote_copy(
            src_ref=src, dst_ref=dst, send_sem=send_sem.at[step, d], recv_sem=recv_sem.at[step, d],
            device_id=(row + dr, col + dc), device_id_type=MESH,
        )

    def start_halo(step):
        for d, (dr, dc) in enumerate(SIDES):
            @pl.when(inside(row + dr, col + dc))
            def _():
                halo(step, d).start()

    def wait_halo(step):
        for d, (dr, dc) in enumerate(SIDES):
            @pl.when(inside(row - dr, col - dc))
            def _():
                halo(step, d).wait_recv()

    def wait_sent(step):
        for d, (dr, dc) in enumerate(SIDES):
            @pl.when(inside(row + dr, col + dc))
            def _():
                halo(step, d).wait_send()

    def kernel_terms(step):
        term = nt(aall[step], zst[step])
        kacc[...] = term if step == steps - 1 else kacc[...] + term

    def emit_inputs(step):
        def put(b, carry):
            at = pl.ds(b * BLOCK, BLOCK)
            gin_out[step, at] = nat[pl.ds((gates + b * BLOCK) * rows, BLOCK * rows), :].reshape(BLOCK, rows, cols).astype(BF16)
            return carry
        lax.fori_loop(0, cin // BLOCK, put, 0)
        store = pltpu.make_async_copy(gin_out.at[step], gin_hbm.at[step], store_sem.at[step])
        store.start()
        stores.append(store)

    def transposed(step):
        product[...] = nn(weight_t[...], aall[step])
        for r in range(rows):
            total = None
            for dr in range(3):
                at = (r + 2 - dr) * cols
                piece = product[dr * width : (dr + 1) * width, at : at + cols]
                total = piece if total is None else total + piece
            gxn = pl.ds(gates * rows + r, cin, stride=rows)
            nat[gxn, :] = total[:cin]
            dhn = pl.ds((gates + cin) * rows + r, hidden, stride=rows)
            nat[dhn, :] = total[cin:]

    bias = None
    stores = []
    for step in reversed(range(steps)):
        last = step == steps - 1

        def backward(b, carry):
            at = pl.ds(b * BLOCK, BLOCK)
            gi, gf, go, gg = (acts[step, n, at] for n in range(4))
            tn = tanhs[step, at]
            err = cot[step, at].astype(F32)
            if not last:
                err = err + nat[pl.ds((gates + cin + b * BLOCK) * rows, BLOCK * rows), :].reshape(BLOCK, rows, cols)
            err = land * err
            dc = gradc[at] + err * go * (1.0 - tn * tn)
            dci = dc * gi
            dcf = dc * gf
            parts = (
                dci * gg * (1.0 - gi),
                dcf * cells[step, at] * (1.0 - gf),
                err * tn * go * (1.0 - go),
                dci * (1.0 - gg * gg),
            )
            for n, value in enumerate(parts):
                nat[pl.ds((n * hidden + b * BLOCK) * rows, BLOCK * rows), :] = value.reshape(BLOCK * rows, cols)
            gradc[at] = dcf
            return carry
        lax.fori_loop(0, hidden // BLOCK, backward, 0)
        for r in range(rows):
            tile = nat[pl.ds(r, gates, stride=rows), :].astype(BF16)
            aall[step, gates : 2 * gates, (r + 1) * cols : (r + 2) * cols] = tile
            bias = tile.astype(F32) if last and r == 0 else bias + tile.astype(F32)
        own = aall[step, gates : 2 * gates, cols : padded - cols]
        picked = nt(selector[...], own).astype(BF16)
        edges[step, 0] = picked[:edge]
        edges[step, 1] = picked[edge:]
        if last:
            pl.semaphore_wait(barrier, number_of_partners(row, col, nrow, ncol, inside))
        start_halo(step)
        if last:
            loads[steps + 2].wait()
            for dr in range(3):
                for dc in range(3):
                    k = 3 * dr + dc
                    weight_t[dr * width : (dr + 1) * width, dc * gates : (dc + 1) * gates] = (
                        weight[:, k * width : (k + 1) * width].astype(F32).T.astype(BF16)
                    )
            loads[steps + 4].wait()
            loads[steps + 5].wait()
            spread(hid)
            place_z(0, cin, hidden)
            for s in range(steps):
                spread(inp, s)
                place_z(s, 0, cin)
        else:
            emit_inputs(step + 1)
            kernel_terms(step + 1)
        wait_halo(step)
        side = nt(identity, border[step]).astype(BF16)
        for j in range(rows + 2):
            at = slice(j * cols, (j + 1) * cols)
            pair = jnp.concatenate([aall[step, gates : 2 * gates, at], side], axis=1)
            moved = nn(pair, shifter[j]).astype(BF16)
            aall[step, 2 * gates : 3 * gates, at] = moved[:, :cols]
            aall[step, 0:gates, at] = moved[:, cols:]
        if step > 0:
            transposed(step)
        wait_sent(step)

    kernel_terms(0)
    for dr in range(3):
        for dc in range(3):
            k = 3 * dr + dc
            kfull[:, k * width : (k + 1) * width] = kacc[dc * gates : (dc + 1) * gates, dr * width : (dr + 1) * width] * scale
    lane = lax.broadcasted_iota(jnp.int32, (gates, lanes), 1)
    tail = lanes - 128

    def split(value):
        block = value[..., tail:]
        at = lax.broadcasted_iota(jnp.int32, block.shape, block.ndim - 1) + tail
        whole = jnp.where(at == part, block + pltpu.roll(block, 127, block.ndim - 1), block)
        own = jnp.where(at == part + 1, 0.0, whole)
        lost = pltpu.roll(own - own.astype(BF16).astype(F32), 1, block.ndim - 1)
        sent = jnp.where(at == part + 1, lost, own).astype(BF16)
        if not tail:
            return own, sent
        rest = value[..., :tail]
        return (
            jnp.concatenate([rest, own], axis=-1),
            jnp.concatenate([rest.astype(BF16), sent], axis=-1),
        )

    bias = jnp.sum(bias, axis=1, keepdims=True) * scale
    for c in range(ncol):
        base, shift = part * c // 128 * 128, part * c % 128
        piece = kfull[:, base : base + lanes + 128]
        if shift:
            piece = pltpu.roll(piece, lanes + 128 - shift, 1)
        piece = jnp.where(lane < part, piece[:, :lanes], jnp.where(lane == part, bias, 0.0))
        sent = split(piece)[1]
        for r in range(nrow):
            kown[r % 2, c, r // 2] = piece[r * high : (r + 1) * high]
            kbuf[r % 2, c, r // 2] = sent[r * high : (r + 1) * high]

    def first():
        return pltpu.make_async_remote_copy(
            src_ref=kbuf.at[1 - core], dst_ref=r1, send_sem=rs_send.at[0], recv_sem=rs_recv.at[0],
            device_id=(sibling, col), device_id_type=MESH,
        )

    def second(j):
        to = (col + j) % ncol
        return pltpu.make_async_remote_copy(
            src_ref=s1.at[to], dst_ref=r2.at[j - 1], send_sem=rs_send.at[j], recv_sem=rs_recv.at[j],
            device_id=(row, to), device_id_type=MESH,
        )

    def third(j):
        to = (zpos + j) % half
        return pltpu.make_async_remote_copy(
            src_ref=s2.at[to], dst_ref=r3.at[j - 1], send_sem=rs_send.at[ncol + j], recv_sem=rs_recv.at[ncol + j],
            device_id=(to * 2 + core, col), device_id_type=MESH,
        )

    first().start()
    transposed(0)
    first().wait_recv()
    for c in range(ncol):
        for z in range(half):
            s1own[c, z], s1[c, z] = split(kown[core, c, z] + r1[c, z].astype(F32))
    for j in range(1, ncol):
        second(j).start()
    emit_inputs(0)
    gh_out[...] = nat[pl.ds((gates + cin) * rows, hidden * rows), :].reshape(hidden, rows, cols)
    gc_out[...] = gradc[...]
    for n, (source, target) in enumerate(((gh_out, gh_hbm), (gc_out, gc_hbm))):
        store = pltpu.make_async_copy(source, target, store_sem.at[steps + n])
        store.start()
        stores.append(store)
    for j in range(1, ncol):
        second(j).wait_recv()
    for z in range(half):
        total = s1own[col, z]
        for j in range(1, ncol):
            total = total + r2[j - 1, z].astype(F32)
        s2own[z], s2[z] = split(total)
    for j in range(1, half):
        third(j).start()
    total = s2own[zpos]
    for j in range(1, half):
        third(j).wait_recv()
        total = total + r3[j - 1].astype(F32)
    gk_out[...] = total[:, :part]
    block = total[:, tail:]
    line = lax.broadcasted_iota(jnp.int32, block.shape, 0)
    lane = lax.broadcasted_iota(jnp.int32, block.shape, 1)
    column = jnp.sum(jnp.where((lane == part - tail) | (lane == part + 1 - tail), block, 0.0), axis=1, keepdims=True)
    each = high // ncol
    wanted = line == lane + col * each
    bias_out[...] = jnp.sum(jnp.where(wanted, column, 0.0), axis=0, keepdims=True)[:, :each]
    for n, (source, target) in enumerate(((gk_out, gk_hbm), (bias_out, bias_hbm))):
        store = pltpu.make_async_copy(source, target, store_sem.at[steps + 2 + n])
        store.start()
        stores.append(store)
    for store in stores:
        store.wait()
    first().wait_send()
    for j in range(1, ncol):
        second(j).wait_send()
    for j in range(1, half):
        third(j).wait_send()


def number_of_partners(row, col, nrow, ncol, inside):
    count = jnp.int32(1 + (ncol - 1) + (nrow // 2 - 1))
    for dr, dc in SIDES:
        count = count + inside(row + dr, col + dc).astype(jnp.int32)
    return count


def finish(*refs):
    sem = refs[-1]
    count = (len(refs) - 1) // 2
    copies = [pltpu.make_async_copy(refs[n], refs[count + n], sem.at[n]) for n in range(count)]
    for copy in copies:
        copy.start()
    for copy in copies:
        copy.wait()


def shards(nrow, ncol, inputs, gate_pre, cotangent, hidden_init, cell_init, land_mask, kernel):
    steps, cin = inputs.shape[:2]
    hidden = hidden_init.shape[0]
    rows, cols = land_mask.shape
    width, gates = cin + hidden, 4 * hidden
    taps = kernel.shape[1]
    padded = (rows + 2) * cols
    edge = -(-rows // 16) * 16
    half, high, part = nrow // 2, gates // nrow, taps // ncol
    lanes = ((part + 1) // 128 + 1) * 128
    plane = (hidden, rows, cols)
    slots = max(half - 1, 1)
    scratch = [
        pltpu.VMEM(inputs.shape, BF16),
        pltpu.VMEM(gate_pre.shape, BF16),
        pltpu.VMEM(cotangent.shape, BF16),
        pltpu.VMEM(plane, BF16),
        pltpu.VMEM(plane, F32),
        pltpu.VMEM((rows, cols), jnp.int32),
        pltpu.VMEM(kernel.shape, BF16),
        pltpu.SemaphoreType.DMA((steps + 6,)),
        pltpu.VMEM((steps, 4) + plane, F32),
        pltpu.VMEM((steps + 1,) + plane, F32),
        pltpu.VMEM((steps,) + plane, F32),
        pltpu.VMEM(plane, F32),
        pltpu.VMEM(((gates + width) * rows, cols), F32),
        pltpu.VMEM((steps, 3 * width, padded), BF16),
        pltpu.VMEM((steps, 3 * gates, padded), BF16),
        pltpu.VMEM((steps, 2, edge, gates), BF16),
        pltpu.VMEM((steps, cols, gates), BF16),
        pltpu.VMEM((rows + 2, 2 * cols, 2 * cols), BF16),
        pltpu.VMEM((3 * width, 3 * gates), BF16),
        pltpu.VMEM((2 * edge, rows * cols), BF16),
        pltpu.VMEM((3 * width, padded), F32),
        pltpu.VMEM((3 * gates, 3 * width), F32),
        pltpu.VMEM((gates, taps + lanes + 128), F32),
        pltpu.VMEM((2, ncol, half, high, lanes), F32),
        pltpu.VMEM((2, ncol, half, high, lanes), BF16),
        pltpu.VMEM((ncol, half, high, lanes), BF16),
        pltpu.VMEM((ncol, half, high, lanes), F32),
        pltpu.VMEM((ncol, half, high, lanes), BF16),
        pltpu.VMEM((ncol - 1, half, high, lanes), BF16),
        pltpu.VMEM((half, high, lanes), F32),
        pltpu.VMEM((half, high, lanes), BF16),
        pltpu.VMEM((slots, high, lanes), BF16),
        pltpu.SemaphoreType.DMA((steps, len(SIDES))),
        pltpu.SemaphoreType.DMA((steps, len(SIDES))),
        pltpu.SemaphoreType.DMA((ncol + half,)),
        pltpu.SemaphoreType.DMA((ncol + half,)),
    ]
    each = high // ncol
    shapes = (
        jax.ShapeDtypeStruct(inputs.shape, BF16),
        jax.ShapeDtypeStruct(plane, F32),
        jax.ShapeDtypeStruct(plane, F32),
        jax.ShapeDtypeStruct((high, part), F32),
        jax.ShapeDtypeStruct((1, each), F32),
    )
    scratch += [pltpu.VMEM(shape.shape, shape.dtype) for shape in shapes]
    scratch.append(pltpu.SemaphoreType.DMA((steps + 4,)))
    hbm = pl.BlockSpec(memory_space=pltpu.HBM)
    results = pl.pallas_call(
        functools.partial(body, (steps, cin, hidden, rows, cols, nrow, ncol)),
        out_shape=shapes,
        in_specs=[hbm] * 7,
        out_specs=[hbm] * 5,
        scratch_shapes=scratch,
        compiler_params=pltpu.CompilerParams(
            collective_id=0, has_side_effects=True, vmem_limit_bytes=60 * 1024 * 1024
        ),
        name="convlstm_backward",
    )(inputs, gate_pre, cotangent, hidden_init, cell_init, land_mask, kernel)
    gin, gh, gc, gk, bias = pl.pallas_call(
        finish,
        out_shape=shapes,
        in_specs=[hbm] * 5,
        out_specs=[hbm] * 5,
        scratch_shapes=[pltpu.SemaphoreType.DMA((5,))],
        compiler_params=pltpu.CompilerParams(vmem_limit_bytes=60 * 1024 * 1024),
        name="write_outputs",
    )(*results)
    return gin, gh, gc, gk, bias.reshape(each)


def solution(mesh):
    placed = (
        P(None, None, "row", "col"),
        P(None, None, "row", "col"),
        P(None, None, "row", "col"),
        P(None, "row", "col"),
        P(None, "row", "col"),
        P("row", "col"),
        P(),
    )
    return jax.shard_map(
        functools.partial(shards, mesh.shape["row"], mesh.shape["col"]),
        mesh=mesh,
        in_specs=placed,
        out_specs=(
            P(None, None, "row", "col"),
            P(None, "row", "col"),
            P(None, "row", "col"),
            P("row", "col"),
            P(("row", "col")),
        ),
        check_vma=False,
    )
```

```python
import functools
import math

import jax
import jax.numpy as jnp
from jax import lax
from jax.experimental import pallas as pl
from jax.experimental.pallas import tpu as pltpu
from jax.sharding import PartitionSpec as P

MESH = pl.DeviceIdType.MESH
F32 = jnp.float32
BF16 = jnp.bfloat16
SIDES = ((-1, 0), (1, 0), (0, 1), (1, 1), (-1, 1), (0, -1), (1, -1), (-1, -1))
BLOCK = 16


def nt(lhs, rhs):
    return lax.dot_general(lhs, rhs, (((1,), (1,)), ((), ())), preferred_element_type=F32)


def nn(lhs, rhs):
    return jnp.dot(lhs, rhs, preferred_element_type=F32)


def sigmoid(value):
    return 0.5 * jnp.tanh(0.5 * value) + 0.5


def body(
    dims,
    inp_in, pre_in, cot_in, hid_in, cell_in, mask_in, weight_in,
    gin_hbm, gh_hbm, gc_hbm, gk_hbm, bias_hbm,
    inp, pre, cot, hid, cell, mask, weight, load_sem,
    acts, cells, tanhs, gradc, nat, zst, aall, edges, border, shifter, weight_t, selector,
    product, kacc, kfull, kown, kbuf, r1, s1own, s1, r2, s2own, s2, r3,
    send_sem, recv_sem, rs_send, rs_recv,
    gin_out, gh_out, gc_out, gk_out, bias_out, store_sem,
):
    steps, cin, hidden, rows, cols, nrow, ncol = dims
    width = cin + hidden
    gates = 4 * hidden
    padded = (rows + 2) * cols
    edge = edges.shape[2]
    half = nrow // 2
    high = gates // nrow
    part = weight.shape[1] // ncol
    lanes = kbuf.shape[-1]
    row, col = lax.axis_index("row"), lax.axis_index("col")
    zpos, core = row // 2, row % 2
    scale = 1.0 / math.sqrt(rows * cols * nrow * ncol)

    def inside(r, c):
        return (r >= 0) & (r < nrow) & (c >= 0) & (c < ncol)

    loads = [pltpu.make_async_copy(pre_in.at[step], pre.at[step], load_sem.at[step]) for step in range(steps)]
    for n, (source, target) in enumerate(
        ((cell_in, cell), (mask_in, mask), (weight_in, weight), (cot_in, cot), (inp_in, inp), (hid_in, hid))
    ):
        loads.append(pltpu.make_async_copy(source, target, load_sem.at[steps + n]))
    for n in (0, steps, steps + 1, steps + 2, *range(1, steps), steps + 3, steps + 4, steps + 5):
        loads[n].start()

    border[...] = jnp.zeros_like(border)
    for step in range(steps):
        aall[step, gates : 2 * gates, 0:cols] = jnp.zeros((gates, cols), BF16)
        aall[step, gates : 2 * gates, padded - cols : padded] = jnp.zeros((gates, cols), BF16)

    barrier = pltpu.get_barrier_semaphore()
    for dr, dc in SIDES:
        @pl.when(inside(row + dr, col + dc))
        def _():
            pl.semaphore_signal(barrier, inc=1, device_id=(row + dr, col + dc), device_id_type=MESH)
    sibling = row + 1 - 2 * core
    pl.semaphore_signal(barrier, inc=1, device_id=(sibling, col), device_id_type=MESH)
    for j in range(1, ncol):
        pl.semaphore_signal(barrier, inc=1, device_id=(row, (col + j) % ncol), device_id_type=MESH)
    for j in range(1, half):
        pl.semaphore_signal(barrier, inc=1, device_id=(((zpos + j) % half) * 2 + core, col), device_id_type=MESH)

    srow = lax.broadcasted_iota(jnp.int32, (2 * cols, 2 * cols), 0)
    scol = lax.broadcasted_iota(jnp.int32, (2 * cols, 2 * cols), 1)
    for j in range(rows + 2):
        if j == 0:
            low, up = edge + rows - 1, 4 * edge + rows - 1
        elif j == rows + 1:
            low, up = 2 * edge, 5 * edge
        else:
            low, up = j - 1, 3 * edge + j - 1
        source = jnp.where(
            scol < cols,
            jnp.where(scol == 0, cols + low, scol - 1),
            jnp.where(scol == 2 * cols - 1, cols + up, scol - cols + 1),
        )
        shifter[j] = (srow == source).astype(F32).astype(BF16)
    prow = lax.broadcasted_iota(jnp.int32, selector.shape, 0)
    pcol = lax.broadcasted_iota(jnp.int32, selector.shape, 1)
    wanted = jnp.where(prow < edge, prow * cols, (prow - edge) * cols + cols - 1)
    valid = (prow % edge) < rows
    selector[...] = ((pcol == wanted) & valid).astype(F32).astype(BF16)
    irow = lax.broadcasted_iota(jnp.int32, (gates, gates), 0)
    icol = lax.broadcasted_iota(jnp.int32, (gates, gates), 1)
    identity = (irow == icol).astype(F32).astype(BF16)

    loads[0].wait()
    loads[steps].wait()
    loads[steps + 1].wait()
    land = mask[...].astype(F32)[None]
    cells[0] = cell[...]
    gradc[...] = jnp.zeros_like(gradc)

    def place_z(step, first, count):
        for r in range(rows):
            tile = nat[pl.ds(r, count, stride=rows), :].astype(BF16)
            for dr in range(3):
                at = (r + 2 - dr) * cols
                zst[step, dr * width + first : dr * width + first + count, at : at + cols] = tile

    for step in range(steps):
        for dr in range(3):
            for i in range(rows + 2):
                if not 0 <= i + dr - 2 < rows:
                    zst[step, dr * width : (dr + 1) * width, i * cols : (i + 1) * cols] = jnp.zeros((width, cols), BF16)

    def spread(ref, step=None):
        def put(b, carry):
            at = pl.ds(b * BLOCK, BLOCK)
            value = (ref[at] if step is None else ref[step, at]).astype(F32)
            nat[pl.ds(b * BLOCK * rows, BLOCK * rows), :] = value.reshape(BLOCK * rows, cols)
            return carry
        lax.fori_loop(0, ref.shape[-3] // BLOCK, put, 0)

    for step in range(steps):
        if step:
            loads[step].wait()

        def forward(b, carry):
            def gate(n):
                return pre[step, pl.ds(n * hidden + b * BLOCK, BLOCK)].astype(F32)
            at = pl.ds(b * BLOCK, BLOCK)
            gi, gf, go, gg = sigmoid(gate(0)), sigmoid(gate(1)), sigmoid(gate(2)), jnp.tanh(gate(3))
            new = gf * cells[step, at] + gi * gg
            tn = jnp.tanh(new)
            acts[step, 0, at] = gi
            acts[step, 1, at] = gf
            acts[step, 2, at] = go
            acts[step, 3, at] = gg
            cells[step + 1, at] = new
            tanhs[step, at] = tn
            nat[pl.ds(b * BLOCK * rows, BLOCK * rows), :] = (land * go * tn).reshape(BLOCK * rows, cols)
            return carry
        lax.fori_loop(0, hidden // BLOCK, forward, 0)
        if step + 1 < steps:
            place_z(step + 1, cin, hidden)

    loads[steps + 3].wait()

    def halo(step, d):
        dr, dc = SIDES[d]
        if dc == 0:
            first = cols if dr < 0 else rows * cols
            land_at = padded - cols if dr < 0 else 0
            src = aall.at[step, pl.ds(gates, gates), pl.ds(first, cols)]
            dst = aall.at[step, pl.ds(gates, gates), pl.ds(land_at, cols)]
        else:
            src = edges.at[step, 1 if dc > 0 else 0]
            dst = border.at[step, pl.ds((d - 2) * edge, edge)]
        return pltpu.make_async_remote_copy(
            src_ref=src, dst_ref=dst, send_sem=send_sem.at[step, d], recv_sem=recv_sem.at[step, d],
            device_id=(row + dr, col + dc), device_id_type=MESH,
        )

    def start_halo(step):
        for d, (dr, dc) in enumerate(SIDES):
            @pl.when(inside(row + dr, col + dc))
            def _():
                halo(step, d).start()

    def wait_halo(step):
        for d, (dr, dc) in enumerate(SIDES):
            @pl.when(inside(row - dr, col - dc))
            def _():
                halo(step, d).wait_recv()

    def wait_sent(step):
        for d, (dr, dc) in enumerate(SIDES):
            @pl.when(inside(row + dr, col + dc))
            def _():
                halo(step, d).wait_send()

    def kernel_terms(step):
        term = nt(aall[step], zst[step])
        kacc[...] = term if step == steps - 1 else kacc[...] + term

    def emit_inputs(step):
        def put(b, carry):
            at = pl.ds(b * BLOCK, BLOCK)
            gin_out[step, at] = nat[pl.ds((gates + b * BLOCK) * rows, BLOCK * rows), :].reshape(BLOCK, rows, cols).astype(BF16)
            return carry
        lax.fori_loop(0, cin // BLOCK, put, 0)
        store = pltpu.make_async_copy(gin_out.at[step], gin_hbm.at[step], store_sem.at[step])
        store.start()
        stores.append(store)

    def transposed(step):
        product[...] = nn(weight_t[...], aall[step])
        for r in range(rows):
            total = None
            for dr in range(3):
                at = (r + 2 - dr) * cols
                piece = product[dr * width : (dr + 1) * width, at : at + cols]
                total = piece if total is None else total + piece
            gxn = pl.ds(gates * rows + r, cin, stride=rows)
            nat[gxn, :] = total[:cin]
            dhn = pl.ds((gates + cin) * rows + r, hidden, stride=rows)
            nat[dhn, :] = total[cin:]

    bias = None
    stores = []
    for step in reversed(range(steps)):
        last = step == steps - 1

        def backward(b, carry):
            at = pl.ds(b * BLOCK, BLOCK)
            gi, gf, go, gg = (acts[step, n, at] for n in range(4))
            tn = tanhs[step, at]
            err = cot[step, at].astype(F32)
            if not last:
                err = err + nat[pl.ds((gates + cin + b * BLOCK) * rows, BLOCK * rows), :].reshape(BLOCK, rows, cols)
            err = land * err
            dc = gradc[at] + err * go * (1.0 - tn * tn)
            dci = dc * gi
            dcf = dc * gf
            parts = (
                dci * gg * (1.0 - gi),
                dcf * cells[step, at] * (1.0 - gf),
                err * tn * go * (1.0 - go),
                dci * (1.0 - gg * gg),
            )
            for n, value in enumerate(parts):
                nat[pl.ds((n * hidden + b * BLOCK) * rows, BLOCK * rows), :] = value.reshape(BLOCK * rows, cols)
            gradc[at] = dcf
            return carry
        lax.fori_loop(0, hidden // BLOCK, backward, 0)
        for r in range(rows):
            tile = nat[pl.ds(r, gates, stride=rows), :].astype(BF16)
            aall[step, gates : 2 * gates, (r + 1) * cols : (r + 2) * cols] = tile
            bias = tile.astype(F32) if last and r == 0 else bias + tile.astype(F32)
        own = aall[step, gates : 2 * gates, cols : padded - cols]
        picked = nt(selector[...], own).astype(BF16)
        edges[step, 0] = picked[:edge]
        edges[step, 1] = picked[edge:]
        if last:
            pl.semaphore_wait(barrier, number_of_partners(row, col, nrow, ncol, inside))
        start_halo(step)
        if last:
            loads[steps + 2].wait()
            for dr in range(3):
                for dc in range(3):
                    k = 3 * dr + dc
                    weight_t[dr * width : (dr + 1) * width, dc * gates : (dc + 1) * gates] = (
                        weight[:, k * width : (k + 1) * width].astype(F32).T.astype(BF16)
                    )
            loads[steps + 4].wait()
            loads[steps + 5].wait()
            spread(hid)
            place_z(0, cin, hidden)
            for s in range(steps):
                spread(inp, s)
                place_z(s, 0, cin)
        else:
            emit_inputs(step + 1)
            kernel_terms(step + 1)
        wait_halo(step)
        side = nt(identity, border[step]).astype(BF16)
        for j in range(rows + 2):
            at = slice(j * cols, (j + 1) * cols)
            pair = jnp.concatenate([aall[step, gates : 2 * gates, at], side], axis=1)
            moved = nn(pair, shifter[j]).astype(BF16)
            aall[step, 2 * gates : 3 * gates, at] = moved[:, :cols]
            aall[step, 0:gates, at] = moved[:, cols:]
        if step > 0:
            transposed(step)
        wait_sent(step)

    kernel_terms(0)
    for dr in range(3):
        for dc in range(3):
            k = 3 * dr + dc
            kfull[:, k * width : (k + 1) * width] = kacc[dc * gates : (dc + 1) * gates, dr * width : (dr + 1) * width] * scale
    lane = lax.broadcasted_iota(jnp.int32, (gates, lanes), 1)
    tail = lanes - 128

    def split(value):
        block = value[..., tail:]
        at = lax.broadcasted_iota(jnp.int32, block.shape, block.ndim - 1) + tail
        whole = jnp.where(at == part, block + pltpu.roll(block, 127, block.ndim - 1), block)
        own = jnp.where(at == part + 1, 0.0, whole)
        lost = pltpu.roll(own - own.astype(BF16).astype(F32), 1, block.ndim - 1)
        sent = jnp.where(at == part + 1, lost, own).astype(BF16)
        if not tail:
            return own, sent
        rest = value[..., :tail]
        return (
            jnp.concatenate([rest, own], axis=-1),
            jnp.concatenate([rest.astype(BF16), sent], axis=-1),
        )

    bias = jnp.sum(bias, axis=1, keepdims=True) * scale
    for c in range(ncol):
        base, shift = part * c // 128 * 128, part * c % 128
        piece = kfull[:, base : base + lanes + 128]
        if shift:
            piece = pltpu.roll(piece, lanes + 128 - shift, 1)
        piece = jnp.where(lane < part, piece[:, :lanes], jnp.where(lane == part, bias, 0.0))
        sent = split(piece)[1]
        for r in range(nrow):
            kown[r % 2, c, r // 2] = piece[r * high : (r + 1) * high]
            kbuf[r % 2, c, r // 2] = sent[r * high : (r + 1) * high]

    def first():
        return pltpu.make_async_remote_copy(
            src_ref=kbuf.at[1 - core], dst_ref=r1, send_sem=rs_send.at[0], recv_sem=rs_recv.at[0],
            device_id=(sibling, col), device_id_type=MESH,
        )

    def second(j):
        to = (col + j) % ncol
        return pltpu.make_async_remote_copy(
            src_ref=s1.at[to], dst_ref=r2.at[j - 1], send_sem=rs_send.at[j], recv_sem=rs_recv.at[j],
            device_id=(row, to), device_id_type=MESH,
        )

    def third(j):
        to = (zpos + j) % half
        return pltpu.make_async_remote_copy(
            src_ref=s2.at[to], dst_ref=r3.at[j - 1], send_sem=rs_send.at[ncol + j], recv_sem=rs_recv.at[ncol + j],
            device_id=(to * 2 + core, col), device_id_type=MESH,
        )

    first().start()
    transposed(0)
    first().wait_recv()
    for c in range(ncol):
        for z in range(half):
            s1own[c, z], s1[c, z] = split(kown[core, c, z] + r1[c, z].astype(F32))
    for j in range(1, ncol):
        second(j).start()
    emit_inputs(0)
    gh_out[...] = nat[pl.ds((gates + cin) * rows, hidden * rows), :].reshape(hidden, rows, cols)
    gc_out[...] = gradc[...]
    for n, (source, target) in enumerate(((gh_out, gh_hbm), (gc_out, gc_hbm))):
        store = pltpu.make_async_copy(source, target, store_sem.at[steps + n])
        store.start()
        stores.append(store)
    for j in range(1, ncol):
        second(j).wait_recv()
    for z in range(half):
        total = s1own[col, z]
        for j in range(1, ncol):
            total = total + r2[j - 1, z].astype(F32)
        s2own[z], s2[z] = split(total)
    for j in range(1, half):
        third(j).start()
    total = s2own[zpos]
    for j in range(1, half):
        third(j).wait_recv()
        total = total + r3[j - 1].astype(F32)
    gk_out[...] = total[:, :part]
    block = total[:, tail:]
    line = lax.broadcasted_iota(jnp.int32, block.shape, 0)
    lane = lax.broadcasted_iota(jnp.int32, block.shape, 1)
    column = jnp.sum(jnp.where((lane == part - tail) | (lane == part + 1 - tail), block, 0.0), axis=1, keepdims=True)
    each = high // ncol
    wanted = line == lane + col * each
    bias_out[...] = jnp.sum(jnp.where(wanted, column, 0.0), axis=0, keepdims=True)[:, :each]
    for n, (source, target) in enumerate(((gk_out, gk_hbm), (bias_out, bias_hbm))):
        store = pltpu.make_async_copy(source, target, store_sem.at[steps + 2 + n])
        store.start()
        stores.append(store)
    for store in stores:
        store.wait()
    first().wait_send()
    for j in range(1, ncol):
        second(j).wait_send()
    for j in range(1, half):
        third(j).wait_send()


def number_of_partners(row, col, nrow, ncol, inside):
    count = jnp.int32(1 + (ncol - 1) + (nrow // 2 - 1))
    for dr, dc in SIDES:
        count = count + inside(row + dr, col + dc).astype(jnp.int32)
    return count


def finish(*refs):
    sem = refs[-1]
    count = (len(refs) - 1) // 3
    sources, targets, held = refs[:count], refs[count : 2 * count], refs[2 * count : 3 * count]
    reads = [pltpu.make_async_copy(sources[n], held[n], sem.at[n]) for n in range(count)]
    writes = [pltpu.make_async_copy(held[n], targets[n], sem.at[count + n]) for n in range(count)]
    for copy in reads:
        copy.start()
    for n in range(count):
        reads[n].wait()
        writes[n].start()
    for copy in writes:
        copy.wait()


def shards(nrow, ncol, inputs, gate_pre, cotangent, hidden_init, cell_init, land_mask, kernel):
    steps, cin = inputs.shape[:2]
    hidden = hidden_init.shape[0]
    rows, cols = land_mask.shape
    width, gates = cin + hidden, 4 * hidden
    taps = kernel.shape[1]
    padded = (rows + 2) * cols
    edge = -(-rows // 16) * 16
    half, high, part = nrow // 2, gates // nrow, taps // ncol
    lanes = ((part + 1) // 128 + 1) * 128
    plane = (hidden, rows, cols)
    slots = max(half - 1, 1)
    scratch = [
        pltpu.VMEM(inputs.shape, BF16),
        pltpu.VMEM(gate_pre.shape, BF16),
        pltpu.VMEM(cotangent.shape, BF16),
        pltpu.VMEM(plane, BF16),
        pltpu.VMEM(plane, F32),
        pltpu.VMEM((rows, cols), jnp.int32),
        pltpu.VMEM(kernel.shape, BF16),
        pltpu.SemaphoreType.DMA((steps + 6,)),
        pltpu.VMEM((steps, 4) + plane, F32),
        pltpu.VMEM((steps + 1,) + plane, F32),
        pltpu.VMEM((steps,) + plane, F32),
        pltpu.VMEM(plane, F32),
        pltpu.VMEM(((gates + width) * rows, cols), F32),
        pltpu.VMEM((steps, 3 * width, padded), BF16),
        pltpu.VMEM((steps, 3 * gates, padded), BF16),
        pltpu.VMEM((steps, 2, edge, gates), BF16),
        pltpu.VMEM((steps, cols, gates), BF16),
        pltpu.VMEM((rows + 2, 2 * cols, 2 * cols), BF16),
        pltpu.VMEM((3 * width, 3 * gates), BF16),
        pltpu.VMEM((2 * edge, rows * cols), BF16),
        pltpu.VMEM((3 * width, padded), F32),
        pltpu.VMEM((3 * gates, 3 * width), F32),
        pltpu.VMEM((gates, taps + lanes + 128), F32),
        pltpu.VMEM((2, ncol, half, high, lanes), F32),
        pltpu.VMEM((2, ncol, half, high, lanes), BF16),
        pltpu.VMEM((ncol, half, high, lanes), BF16),
        pltpu.VMEM((ncol, half, high, lanes), F32),
        pltpu.VMEM((ncol, half, high, lanes), BF16),
        pltpu.VMEM((ncol - 1, half, high, lanes), BF16),
        pltpu.VMEM((half, high, lanes), F32),
        pltpu.VMEM((half, high, lanes), BF16),
        pltpu.VMEM((slots, high, lanes), BF16),
        pltpu.SemaphoreType.DMA((steps, len(SIDES))),
        pltpu.SemaphoreType.DMA((steps, len(SIDES))),
        pltpu.SemaphoreType.DMA((ncol + half,)),
        pltpu.SemaphoreType.DMA((ncol + half,)),
    ]
    each = high // ncol
    shapes = (
        jax.ShapeDtypeStruct(inputs.shape, BF16),
        jax.ShapeDtypeStruct(plane, F32),
        jax.ShapeDtypeStruct(plane, F32),
        jax.ShapeDtypeStruct((high, part), F32),
        jax.ShapeDtypeStruct((1, each), F32),
    )
    scratch += [pltpu.VMEM(shape.shape, shape.dtype) for shape in shapes]
    scratch.append(pltpu.SemaphoreType.DMA((steps + 4,)))
    hbm = pl.BlockSpec(memory_space=pltpu.HBM)
    results = pl.pallas_call(
        functools.partial(body, (steps, cin, hidden, rows, cols, nrow, ncol)),
        out_shape=shapes,
        in_specs=[hbm] * 7,
        out_specs=[hbm] * 5,
        scratch_shapes=scratch,
        compiler_params=pltpu.CompilerParams(
            collective_id=0, has_side_effects=True, vmem_limit_bytes=60 * 1024 * 1024
        ),
        name="convlstm_backward",
    )(inputs, gate_pre, cotangent, hidden_init, cell_init, land_mask, kernel)
    gin, gh, gc, gk, bias = pl.pallas_call(
        finish,
        out_shape=shapes,
        in_specs=[hbm] * 5,
        out_specs=[hbm] * 5,
        scratch_shapes=[pltpu.VMEM(shape.shape, shape.dtype) for shape in shapes] + [pltpu.SemaphoreType.DMA((10,))],
        compiler_params=pltpu.CompilerParams(vmem_limit_bytes=60 * 1024 * 1024),
        name="write_outputs",
    )(*results)
    return gin, gh, gc, gk, bias.reshape(each)


def solution(mesh):
    placed = (
        P(None, None, "row", "col"),
        P(None, None, "row", "col"),
        P(None, None, "row", "col"),
        P(None, "row", "col"),
        P(None, "row", "col"),
        P("row", "col"),
        P(),
    )
    return jax.shard_map(
        functools.partial(shards, mesh.shape["row"], mesh.shape["col"]),
        mesh=mesh,
        in_specs=placed,
        out_specs=(
            P(None, None, "row", "col"),
            P(None, "row", "col"),
            P(None, "row", "col"),
            P("row", "col"),
            P(("row", "col")),
        ),
        check_vma=False,
    )
```

```python
import functools
import math

import jax
import jax.numpy as jnp
from jax import lax
from jax.experimental import pallas as pl
from jax.experimental.pallas import tpu as pltpu
from jax.sharding import PartitionSpec as P

MESH = pl.DeviceIdType.MESH
F32 = jnp.float32
BF16 = jnp.bfloat16
SIDES = ((-1, 0), (1, 0), (0, 1), (1, 1), (-1, 1), (0, -1), (1, -1), (-1, -1))
BLOCK = 16


def nt(lhs, rhs):
    return lax.dot_general(lhs, rhs, (((1,), (1,)), ((), ())), preferred_element_type=F32)


def nn(lhs, rhs):
    return jnp.dot(lhs, rhs, preferred_element_type=F32)


def sigmoid(value):
    return 0.5 * jnp.tanh(0.5 * value) + 0.5


def body(
    dims,
    inp_in, pre_in, cot_in, hid_in, cell_in, mask_in, weight_in,
    gin_hbm, gh_hbm, gc_hbm, gk_hbm, bias_hbm,
    inp, pre, cot, hid, cell, mask, weight, load_sem,
    acts, cells, tanhs, gradc, nat, zwin, zedges, zborder, aall, edges, border, shifter, colsel, weight_t, selector,
    product, ymain, kfull, kown, kbuf, r1, s1own, s1, r2, s2own, s2, r3,
    send_sem, recv_sem, rs_send, rs_recv,
    gin_out, gh_out, gc_out, gk_out, bias_out, store_sem,
):
    steps, cin, hidden, rows, cols, nrow, ncol = dims
    width = cin + hidden
    gates = 4 * hidden
    padded = (rows + 2) * cols
    edge = edges.shape[2]
    half = nrow // 2
    high = gates // nrow
    part = weight.shape[1] // ncol
    lanes = kbuf.shape[-1]
    row, col = lax.axis_index("row"), lax.axis_index("col")
    zpos, core = row // 2, row % 2
    scale = 1.0 / math.sqrt(rows * cols * nrow * ncol)

    def inside(r, c):
        return (r >= 0) & (r < nrow) & (c >= 0) & (c < ncol)

    loads = [pltpu.make_async_copy(pre_in.at[step], pre.at[step], load_sem.at[step]) for step in range(steps)]
    for n, (source, target) in enumerate(
        ((cell_in, cell), (mask_in, mask), (weight_in, weight), (cot_in, cot), (inp_in, inp), (hid_in, hid))
    ):
        loads.append(pltpu.make_async_copy(source, target, load_sem.at[steps + n]))
    for n in (0, steps, steps + 1, steps + 2, *range(1, steps), steps + 3, steps + 4, steps + 5):
        loads[n].start()

    border[...] = jnp.zeros_like(border)
    for step in range(steps):
        aall[step, gates : 2 * gates, 0:cols] = jnp.zeros((gates, cols), BF16)
        aall[step, gates : 2 * gates, padded - cols : padded] = jnp.zeros((gates, cols), BF16)
        zwin[step, width : 2 * width, 0:cols] = jnp.zeros((width, cols), BF16)
        zwin[step, width : 2 * width, padded - cols : padded] = jnp.zeros((width, cols), BF16)
    zborder[...] = jnp.zeros_like(zborder)

    barrier = pltpu.get_barrier_semaphore()
    for dr, dc in SIDES:
        @pl.when(inside(row + dr, col + dc))
        def _():
            pl.semaphore_signal(barrier, inc=1, device_id=(row + dr, col + dc), device_id_type=MESH)
    sibling = row + 1 - 2 * core
    pl.semaphore_signal(barrier, inc=1, device_id=(sibling, col), device_id_type=MESH)
    for j in range(1, ncol):
        pl.semaphore_signal(barrier, inc=1, device_id=(row, (col + j) % ncol), device_id_type=MESH)
    for j in range(1, half):
        pl.semaphore_signal(barrier, inc=1, device_id=(((zpos + j) % half) * 2 + core, col), device_id_type=MESH)

    srow = lax.broadcasted_iota(jnp.int32, (2 * cols, 2 * cols), 0)
    scol = lax.broadcasted_iota(jnp.int32, (2 * cols, 2 * cols), 1)
    for j in range(rows + 2):
        if j == 0:
            low, up = edge + rows - 1, 4 * edge + rows - 1
        elif j == rows + 1:
            low, up = 2 * edge, 5 * edge
        else:
            low, up = j - 1, 3 * edge + j - 1
        source = jnp.where(
            scol < cols,
            jnp.where(scol == 0, cols + low, scol - 1),
            jnp.where(scol == 2 * cols - 1, cols + up, scol - cols + 1),
        )
        shifter[j] = (srow == source).astype(F32).astype(BF16)
    prow = lax.broadcasted_iota(jnp.int32, selector.shape, 0)
    pcol = lax.broadcasted_iota(jnp.int32, selector.shape, 1)
    wanted = jnp.where(prow < edge, prow * cols, (prow - edge) * cols + cols - 1)
    valid = (prow % edge) < rows
    selector[...] = ((pcol == wanted) & valid).astype(F32).astype(BF16)
    gap = cols // rows
    crow = lax.broadcasted_iota(jnp.int32, (cols, cols), 0)
    ccol = lax.broadcasted_iota(jnp.int32, (cols, cols), 1)
    for side in range(2):
        at = crow if side == 0 else (crow + 1) % cols
        for dr in range(3):
            j = at // gap + 2 - dr
            near = side * 3 * edge
            source = jnp.where(j == 0, near + edge + rows - 1, jnp.where(j == rows + 1, near + 2 * edge, near + j - 1))
            n = side * 3 + dr
            colsel[n * cols : (n + 1) * cols] = ((ccol == source) & (at % gap == 0)).astype(F32).astype(BF16)
    irow = lax.broadcasted_iota(jnp.int32, (width, width), 0)
    icol = lax.broadcasted_iota(jnp.int32, (width, width), 1)
    identity = (irow == icol).astype(F32).astype(BF16)

    loads[0].wait()
    loads[steps].wait()
    loads[steps + 1].wait()
    land = mask[...].astype(F32)[None]
    cells[0] = cell[...]
    gradc[...] = jnp.zeros_like(gradc)

    def place_z(step, first, count):
        for r in range(rows):
            tile = nat[pl.ds(r, count, stride=rows), :].astype(BF16)
            zwin[step, width + first : width + first + count, (r + 1) * cols : (r + 2) * cols] = tile

    def spread(ref, step=None):
        def put(b, carry):
            at = pl.ds(b * BLOCK, BLOCK)
            value = (ref[at] if step is None else ref[step, at]).astype(F32)
            nat[pl.ds(b * BLOCK * rows, BLOCK * rows), :] = value.reshape(BLOCK * rows, cols)
            return carry
        lax.fori_loop(0, ref.shape[-3] // BLOCK, put, 0)

    for step in range(steps):
        if step:
            loads[step].wait()

        def forward(b, carry):
            def gate(n):
                return pre[step, pl.ds(n * hidden + b * BLOCK, BLOCK)].astype(F32)
            at = pl.ds(b * BLOCK, BLOCK)
            gi, gf, go, gg = sigmoid(gate(0)), sigmoid(gate(1)), sigmoid(gate(2)), jnp.tanh(gate(3))
            new = gf * cells[step, at] + gi * gg
            tn = jnp.tanh(new)
            acts[step, 0, at] = gi
            acts[step, 1, at] = gf
            acts[step, 2, at] = go
            acts[step, 3, at] = gg
            cells[step + 1, at] = new
            tanhs[step, at] = tn
            nat[pl.ds(b * BLOCK * rows, BLOCK * rows), :] = (land * go * tn).reshape(BLOCK * rows, cols)
            return carry
        lax.fori_loop(0, hidden // BLOCK, forward, 0)
        if step + 1 < steps:
            place_z(step + 1, cin, hidden)

    loads[steps + 3].wait()

    def halo(step, d):
        dr, dc = SIDES[d]
        if dc == 0 and step == steps:
            first = cols if dr < 0 else rows * cols
            land_at = padded - cols if dr < 0 else 0
            src = zwin.at[:, pl.ds(width, width), pl.ds(first, cols)]
            dst = zwin.at[:, pl.ds(width, width), pl.ds(land_at, cols)]
        elif step == steps:
            src = zedges.at[1 if dc > 0 else 0]
            dst = zborder.at[pl.ds((d - 2) * edge, edge)]
        elif dc == 0:
            first = cols if dr < 0 else rows * cols
            land_at = padded - cols if dr < 0 else 0
            src = aall.at[step, pl.ds(gates, gates), pl.ds(first, cols)]
            dst = aall.at[step, pl.ds(gates, gates), pl.ds(land_at, cols)]
        else:
            src = edges.at[step, 1 if dc > 0 else 0]
            dst = border.at[step, pl.ds((d - 2) * edge, edge)]
        return pltpu.make_async_remote_copy(
            src_ref=src, dst_ref=dst, send_sem=send_sem.at[step, d], recv_sem=recv_sem.at[step, d],
            device_id=(row + dr, col + dc), device_id_type=MESH,
        )

    def start_halo(step):
        for d, (dr, dc) in enumerate(SIDES):
            @pl.when(inside(row + dr, col + dc))
            def _():
                halo(step, d).start()

    def wait_halo(step):
        for d, (dr, dc) in enumerate(SIDES):
            @pl.when(inside(row - dr, col - dc))
            def _():
                halo(step, d).wait_recv()

    def wait_sent(step):
        for d, (dr, dc) in enumerate(SIDES):
            @pl.when(inside(row + dr, col + dc))
            def _():
                halo(step, d).wait_send()

    def kernel_terms(step):
        own = aall[step, gates : 2 * gates, cols : padded - cols]
        for dr in range(3):
            at = slice(dr * 3 * width, (dr + 1) * 3 * width)
            term = nt(own, zwin[step, :, dr * cols : (dr + rows) * cols])
            kfull[:, at] = term if step == steps - 1 else kfull[:, at] + term

    def z_edges():
        for s in range(steps):
            picked = nt(selector[...], zwin[s, width : 2 * width, cols : padded - cols]).astype(BF16)
            zedges[0, :, s * width : (s + 1) * width] = picked[:edge]
            zedges[1, :, s * width : (s + 1) * width] = picked[edge:]

    def z_windows():
        sides = [nt(identity, zborder[:, s * width : (s + 1) * width]).astype(BF16) for s in range(steps)]
        for j in range(rows + 2):
            at = slice(j * cols, (j + 1) * cols)
            pairs = jnp.concatenate(
                [jnp.concatenate([zwin[s, width : 2 * width, at], sides[s]], axis=1) for s in range(steps)], axis=0
            )
            moved = nn(pairs, shifter[j]).astype(BF16)
            for s in range(steps):
                zwin[s, 0:width, at] = moved[s * width : (s + 1) * width, :cols]
                zwin[s, 2 * width : 3 * width, at] = moved[s * width : (s + 1) * width, cols:]

    def emit_inputs(step):
        def put(b, carry):
            at = pl.ds(b * BLOCK, BLOCK)
            gin_out[step, at] = nat[pl.ds((gates + b * BLOCK) * rows, BLOCK * rows), :].reshape(BLOCK, rows, cols).astype(BF16)
            return carry
        lax.fori_loop(0, cin // BLOCK, put, 0)
        store = pltpu.make_async_copy(gin_out.at[step], gin_hbm.at[step], store_sem.at[step])
        store.start()
        stores.append(store)

    def shift_row(step, j):
        at = slice(j * cols, (j + 1) * cols)
        moved = nn(aall[step, gates : 2 * gates, at], shifter[1, :cols]).astype(BF16)
        aall[step, 2 * gates : 3 * gates, at] = moved[:, :cols]
        aall[step, 0:gates, at] = moved[:, cols:]

    def transposed_own(step):
        for r in range(rows):
            shift_row(step, r + 1)
        product[...] = nn(weight_t[...], aall[step, :, cols : padded - cols])
        for r in range(rows):
            total = None
            for dr in range(3):
                if 0 <= r + 1 - dr < rows:
                    at = (r + 1 - dr) * cols
                    piece = product[dr * width : (dr + 1) * width, at : at + cols]
                    total = piece if total is None else total + piece
            ymain[:, r * cols : (r + 1) * cols] = total

    def transposed_halo(step):
        shift_row(step, 0)
        shift_row(step, rows + 1)
        above = nn(weight_t[2 * width : 3 * width], aall[step, :, 0:cols])
        below = nn(weight_t[0:width], aall[step, :, padded - cols : padded])
        picked = nn(colsel[...], border[step]).astype(BF16)
        sides = None
        for side in range(2):
            for dr in range(3):
                n, k = side * 3 + dr, 3 * dr + 2 - 2 * side
                piece = nn(picked[n * cols : (n + 1) * cols], weight[:, k * width : (k + 1) * width])
                sides = piece if sides is None else sides + piece
        sides = sides.T
        lane = lax.broadcasted_iota(jnp.int32, (width, cols), 1)
        outer = (lane == 0) | (lane == cols - 1)
        for r in range(rows):
            moved = pltpu.roll(sides, cols - gap * r, 1) if r else sides
            total = ymain[:, r * cols : (r + 1) * cols] + jnp.where(outer, moved, 0.0)
            if r == 0:
                total = total + above
            if r == rows - 1:
                total = total + below
            nat[pl.ds(gates * rows + r, cin, stride=rows), :] = total[:cin]
            nat[pl.ds((gates + cin) * rows + r, hidden, stride=rows), :] = total[cin:]

    bias = None
    stores = []
    for step in reversed(range(steps)):
        last = step == steps - 1

        def backward(b, carry):
            at = pl.ds(b * BLOCK, BLOCK)
            gi, gf, go, gg = (acts[step, n, at] for n in range(4))
            tn = tanhs[step, at]
            err = cot[step, at].astype(F32)
            if not last:
                err = err + nat[pl.ds((gates + cin + b * BLOCK) * rows, BLOCK * rows), :].reshape(BLOCK, rows, cols)
            err = land * err
            dc = gradc[at] + err * go * (1.0 - tn * tn)
            dci = dc * gi
            dcf = dc * gf
            parts = (
                dci * gg * (1.0 - gi),
                dcf * cells[step, at] * (1.0 - gf),
                err * tn * go * (1.0 - go),
                dci * (1.0 - gg * gg),
            )
            for n, value in enumerate(parts):
                nat[pl.ds((n * hidden + b * BLOCK) * rows, BLOCK * rows), :] = value.reshape(BLOCK * rows, cols)
            gradc[at] = dcf
            return carry
        lax.fori_loop(0, hidden // BLOCK, backward, 0)
        for r in range(rows):
            tile = nat[pl.ds(r, gates, stride=rows), :].astype(BF16)
            aall[step, gates : 2 * gates, (r + 1) * cols : (r + 2) * cols] = tile
            bias = tile.astype(F32) if last and r == 0 else bias + tile.astype(F32)
        own = aall[step, gates : 2 * gates, cols : padded - cols]
        picked = nt(selector[...], own).astype(BF16)
        edges[step, 0] = picked[:edge]
        edges[step, 1] = picked[edge:]
        if last:
            pl.semaphore_wait(barrier, number_of_partners(row, col, nrow, ncol, inside))
        start_halo(step)
        if last:
            loads[steps + 2].wait()
            for dr in range(3):
                for dc in range(3):
                    k = 3 * dr + dc
                    weight_t[dr * width : (dr + 1) * width, dc * gates : (dc + 1) * gates] = (
                        weight[:, k * width : (k + 1) * width].astype(F32).T.astype(BF16)
                    )
            transposed_own(step)
            loads[steps + 4].wait()
            loads[steps + 5].wait()
            spread(hid)
            place_z(0, cin, hidden)
            for s in range(steps):
                spread(inp, s)
                place_z(s, 0, cin)
            z_edges()
            start_halo(steps)
        elif step > 0:
            transposed_own(step)
            emit_inputs(step + 1)
            if step == steps - 2:
                wait_halo(steps)
                z_windows()
                kernel_terms(steps - 1)
            kernel_terms(step)
        else:
            kernel_terms(0)
        if step > 0:
            wait_halo(step)
            transposed_halo(step)

    lane = lax.broadcasted_iota(jnp.int32, (gates, lanes), 1)
    tail = lanes - 128

    def split(value):
        block = value[..., tail:]
        at = lax.broadcasted_iota(jnp.int32, block.shape, block.ndim - 1) + tail
        whole = jnp.where(at == part, block + pltpu.roll(block, 127, block.ndim - 1), block)
        own = jnp.where(at == part + 1, 0.0, whole)
        lost = pltpu.roll(own - own.astype(BF16).astype(F32), 1, block.ndim - 1)
        sent = jnp.where(at == part + 1, lost, own).astype(BF16)
        if not tail:
            return own, sent
        rest = value[..., :tail]
        return (
            jnp.concatenate([rest, own], axis=-1),
            jnp.concatenate([rest.astype(BF16), sent], axis=-1),
        )

    bias = jnp.sum(bias, axis=1, keepdims=True) * scale
    for c in range(ncol):
        base, shift = part * c // 128 * 128, part * c % 128
        piece = kfull[:, base : base + lanes + 128]
        if shift:
            piece = pltpu.roll(piece, lanes + 128 - shift, 1)
        piece = jnp.where(lane < part, piece[:, :lanes] * scale, jnp.where(lane == part, bias, 0.0))
        sent = split(piece)[1]
        for r in range(nrow):
            kown[r % 2, c, r // 2] = piece[r * high : (r + 1) * high]
            kbuf[r % 2, c, r // 2] = sent[r * high : (r + 1) * high]

    def first():
        return pltpu.make_async_remote_copy(
            src_ref=kbuf.at[1 - core], dst_ref=r1, send_sem=rs_send.at[0], recv_sem=rs_recv.at[0],
            device_id=(sibling, col), device_id_type=MESH,
        )

    def second(j):
        to = (col + j) % ncol
        return pltpu.make_async_remote_copy(
            src_ref=s1.at[to], dst_ref=r2.at[j - 1], send_sem=rs_send.at[j], recv_sem=rs_recv.at[j],
            device_id=(row, to), device_id_type=MESH,
        )

    def third(j):
        to = (zpos + j) % half
        return pltpu.make_async_remote_copy(
            src_ref=s2.at[to], dst_ref=r3.at[j - 1], send_sem=rs_send.at[ncol + j], recv_sem=rs_recv.at[ncol + j],
            device_id=(to * 2 + core, col), device_id_type=MESH,
        )

    first().start()
    transposed_own(0)
    if steps > 1:
        emit_inputs(1)
    wait_halo(0)
    transposed_halo(0)
    first().wait_recv()
    for c in range(ncol):
        for z in range(half):
            s1own[c, z], s1[c, z] = split(kown[core, c, z] + r1[c, z].astype(F32))
    for j in range(1, ncol):
        second(j).start()
    emit_inputs(0)
    gh_out[...] = nat[pl.ds((gates + cin) * rows, hidden * rows), :].reshape(hidden, rows, cols)
    gc_out[...] = gradc[...]
    for n, (source, target) in enumerate(((gh_out, gh_hbm), (gc_out, gc_hbm))):
        store = pltpu.make_async_copy(source, target, store_sem.at[steps + n])
        store.start()
        stores.append(store)
    for j in range(1, ncol):
        second(j).wait_recv()
    for z in range(half):
        total = s1own[col, z]
        for j in range(1, ncol):
            total = total + r2[j - 1, z].astype(F32)
        s2own[z], s2[z] = split(total)
    for j in range(1, half):
        third(j).start()
    total = s2own[zpos]
    for j in range(1, half):
        third(j).wait_recv()
        total = total + r3[j - 1].astype(F32)
    gk_out[...] = total[:, :part]
    block = total[:, tail:]
    line = lax.broadcasted_iota(jnp.int32, block.shape, 0)
    lane = lax.broadcasted_iota(jnp.int32, block.shape, 1)
    column = jnp.sum(jnp.where((lane == part - tail) | (lane == part + 1 - tail), block, 0.0), axis=1, keepdims=True)
    each = high // ncol
    wanted = line == lane + col * each
    bias_out[...] = jnp.sum(jnp.where(wanted, column, 0.0), axis=0, keepdims=True)[:, :each]
    for n, (source, target) in enumerate(((gk_out, gk_hbm), (bias_out, bias_hbm))):
        store = pltpu.make_async_copy(source, target, store_sem.at[steps + 2 + n])
        store.start()
        stores.append(store)
    for store in stores:
        store.wait()
    for step in range(steps + 1):
        wait_sent(step)
    first().wait_send()
    for j in range(1, ncol):
        second(j).wait_send()
    for j in range(1, half):
        third(j).wait_send()


def number_of_partners(row, col, nrow, ncol, inside):
    count = jnp.int32(1 + (ncol - 1) + (nrow // 2 - 1))
    for dr, dc in SIDES:
        count = count + inside(row + dr, col + dc).astype(jnp.int32)
    return count


def finish(*refs):
    sem = refs[-1]
    count = (len(refs) - 1) // 3
    sources, targets, held = refs[:count], refs[count : 2 * count], refs[2 * count : 3 * count]
    reads = [pltpu.make_async_copy(sources[n], held[n], sem.at[n]) for n in range(count)]
    writes = [pltpu.make_async_copy(held[n], targets[n], sem.at[count + n]) for n in range(count)]
    for copy in reads:
        copy.start()
    for n in range(count):
        reads[n].wait()
        writes[n].start()
    for copy in writes:
        copy.wait()


def shards(nrow, ncol, inputs, gate_pre, cotangent, hidden_init, cell_init, land_mask, kernel):
    steps, cin = inputs.shape[:2]
    hidden = hidden_init.shape[0]
    rows, cols = land_mask.shape
    width, gates = cin + hidden, 4 * hidden
    taps = kernel.shape[1]
    padded = (rows + 2) * cols
    edge = -(-rows // 16) * 16
    half, high, part = nrow // 2, gates // nrow, taps // ncol
    lanes = ((part + 1) // 128 + 1) * 128
    plane = (hidden, rows, cols)
    slots = max(half - 1, 1)
    scratch = [
        pltpu.VMEM(inputs.shape, BF16),
        pltpu.VMEM(gate_pre.shape, BF16),
        pltpu.VMEM(cotangent.shape, BF16),
        pltpu.VMEM(plane, BF16),
        pltpu.VMEM(plane, F32),
        pltpu.VMEM((rows, cols), jnp.int32),
        pltpu.VMEM(kernel.shape, BF16),
        pltpu.SemaphoreType.DMA((steps + 6,)),
        pltpu.VMEM((steps, 4) + plane, F32),
        pltpu.VMEM((steps + 1,) + plane, F32),
        pltpu.VMEM((steps,) + plane, F32),
        pltpu.VMEM(plane, F32),
        pltpu.VMEM(((gates + width) * rows, cols), F32),
        pltpu.VMEM((steps, 3 * width, padded), BF16),
        pltpu.VMEM((2, edge, steps * width), BF16),
        pltpu.VMEM((cols, steps * width), BF16),
        pltpu.VMEM((steps, 3 * gates, padded), BF16),
        pltpu.VMEM((steps, 2, edge, gates), BF16),
        pltpu.VMEM((steps, cols, gates), BF16),
        pltpu.VMEM((rows + 2, 2 * cols, 2 * cols), BF16),
        pltpu.VMEM((6 * cols, cols), BF16),
        pltpu.VMEM((3 * width, 3 * gates), BF16),
        pltpu.VMEM((2 * edge, rows * cols), BF16),
        pltpu.VMEM((3 * width, rows * cols), F32),
        pltpu.VMEM((width, rows * cols), F32),
        pltpu.VMEM((gates, taps + lanes + 128), F32),
        pltpu.VMEM((2, ncol, half, high, lanes), F32),
        pltpu.VMEM((2, ncol, half, high, lanes), BF16),
        pltpu.VMEM((ncol, half, high, lanes), BF16),
        pltpu.VMEM((ncol, half, high, lanes), F32),
        pltpu.VMEM((ncol, half, high, lanes), BF16),
        pltpu.VMEM((ncol - 1, half, high, lanes), BF16),
        pltpu.VMEM((half, high, lanes), F32),
        pltpu.VMEM((half, high, lanes), BF16),
        pltpu.VMEM((slots, high, lanes), BF16),
        pltpu.SemaphoreType.DMA((steps + 1, len(SIDES))),
        pltpu.SemaphoreType.DMA((steps + 1, len(SIDES))),
        pltpu.SemaphoreType.DMA((ncol + half,)),
        pltpu.SemaphoreType.DMA((ncol + half,)),
    ]
    each = high // ncol
    shapes = (
        jax.ShapeDtypeStruct(inputs.shape, BF16),
        jax.ShapeDtypeStruct(plane, F32),
        jax.ShapeDtypeStruct(plane, F32),
        jax.ShapeDtypeStruct((high, part), F32),
        jax.ShapeDtypeStruct((1, each), F32),
    )
    scratch += [pltpu.VMEM(shape.shape, shape.dtype) for shape in shapes]
    scratch.append(pltpu.SemaphoreType.DMA((steps + 4,)))
    hbm = pl.BlockSpec(memory_space=pltpu.HBM)
    results = pl.pallas_call(
        functools.partial(body, (steps, cin, hidden, rows, cols, nrow, ncol)),
        out_shape=shapes,
        in_specs=[hbm] * 7,
        out_specs=[hbm] * 5,
        scratch_shapes=scratch,
        compiler_params=pltpu.CompilerParams(
            collective_id=0, has_side_effects=True, vmem_limit_bytes=60 * 1024 * 1024
        ),
        name="convlstm_backward",
    )(inputs, gate_pre, cotangent, hidden_init, cell_init, land_mask, kernel)
    gin, gh, gc, gk, bias = pl.pallas_call(
        finish,
        out_shape=shapes,
        in_specs=[hbm] * 5,
        out_specs=[hbm] * 5,
        scratch_shapes=[pltpu.VMEM(shape.shape, shape.dtype) for shape in shapes] + [pltpu.SemaphoreType.DMA((10,))],
        compiler_params=pltpu.CompilerParams(vmem_limit_bytes=60 * 1024 * 1024),
        name="write_outputs",
    )(*results)
    return gin, gh, gc, gk, bias.reshape(each)


def solution(mesh):
    placed = (
        P(None, None, "row", "col"),
        P(None, None, "row", "col"),
        P(None, None, "row", "col"),
        P(None, "row", "col"),
        P(None, "row", "col"),
        P("row", "col"),
        P(),
    )
    return jax.shard_map(
        functools.partial(shards, mesh.shape["row"], mesh.shape["col"]),
        mesh=mesh,
        in_specs=placed,
        out_specs=(
            P(None, None, "row", "col"),
            P(None, "row", "col"),
            P(None, "row", "col"),
            P("row", "col"),
            P(("row", "col")),
        ),
        check_vma=False,
    )
```

```python
import functools
import math

import jax
import jax.numpy as jnp
from jax import lax
from jax.experimental import pallas as pl
from jax.experimental.pallas import tpu as pltpu
from jax.sharding import PartitionSpec as P

MESH = pl.DeviceIdType.MESH
F32 = jnp.float32
BF16 = jnp.bfloat16
SIDES = ((-1, 0), (1, 0), (0, 1), (1, 1), (-1, 1), (0, -1), (1, -1), (-1, -1))
BLOCK = 16


def nt(lhs, rhs):
    return lax.dot_general(lhs, rhs, (((1,), (1,)), ((), ())), preferred_element_type=F32)


def nn(lhs, rhs):
    return jnp.dot(lhs, rhs, preferred_element_type=F32)


def sigmoid(value):
    return 0.5 * jnp.tanh(0.5 * value) + 0.5


def body(
    dims,
    inp_in, pre_in, cot_in, hid_in, cell_in, mask_in, weight_in,
    gin_hbm, gh_hbm, gc_hbm, gk_hbm, bias_hbm,
    inp, pre, cot, hid, cell, mask, weight, load_sem,
    acts, cells, tanhs, gradc, nat, zwin, zedges, zborder, aall, edges, border, shifter, colsel, weight_t, selector,
    product, ymain, kfull, kown, kbuf, r1, s1own, s1, r2, s2own, s2, r3,
    send_sem, recv_sem, one_send, one_recv, two_send, two_recv, three_send, three_recv,
    gin_out, gh_out, gc_out, gk_out, bias_out, store_sem,
):
    steps, cin, hidden, rows, cols, nrow, ncol = dims
    width = cin + hidden
    gates = 4 * hidden
    padded = (rows + 2) * cols
    edge = edges.shape[2]
    half = nrow // 2
    high = gates // nrow
    part = weight.shape[1] // ncol
    lanes = kbuf.shape[-1]
    row, col = lax.axis_index("row"), lax.axis_index("col")
    zpos, core = row // 2, row % 2
    scale = 1.0 / math.sqrt(rows * cols * nrow * ncol)

    def inside(r, c):
        return (r >= 0) & (r < nrow) & (c >= 0) & (c < ncol)

    loads = [pltpu.make_async_copy(pre_in.at[step], pre.at[step], load_sem.at[step]) for step in range(steps)]
    for n, (source, target) in enumerate(
        ((cell_in, cell), (mask_in, mask), (weight_in, weight), (cot_in, cot), (inp_in, inp), (hid_in, hid))
    ):
        loads.append(pltpu.make_async_copy(source, target, load_sem.at[steps + n]))
    for n in (0, steps, steps + 1, steps + 2, *range(1, steps), steps + 3, steps + 4, steps + 5):
        loads[n].start()

    border[...] = jnp.zeros_like(border)
    for step in range(steps):
        aall[step, gates : 2 * gates, 0:cols] = jnp.zeros((gates, cols), BF16)
        aall[step, gates : 2 * gates, padded - cols : padded] = jnp.zeros((gates, cols), BF16)
        zwin[step, width : 2 * width, 0:cols] = jnp.zeros((width, cols), BF16)
        zwin[step, width : 2 * width, padded - cols : padded] = jnp.zeros((width, cols), BF16)
    zborder[...] = jnp.zeros_like(zborder)

    barrier = pltpu.get_barrier_semaphore()
    for dr, dc in SIDES:
        @pl.when(inside(row + dr, col + dc))
        def _():
            pl.semaphore_signal(barrier, inc=1, device_id=(row + dr, col + dc), device_id_type=MESH)
    sibling = row + 1 - 2 * core
    pl.semaphore_signal(barrier, inc=1, device_id=(sibling, col), device_id_type=MESH)
    for j in range(1, ncol):
        pl.semaphore_signal(barrier, inc=1, device_id=(row, (col + j) % ncol), device_id_type=MESH)
    for j in range(1, half):
        pl.semaphore_signal(barrier, inc=1, device_id=(((zpos + j) % half) * 2 + core, col), device_id_type=MESH)

    srow = lax.broadcasted_iota(jnp.int32, (2 * cols, 2 * cols), 0)
    scol = lax.broadcasted_iota(jnp.int32, (2 * cols, 2 * cols), 1)
    for j in range(rows + 2):
        if j == 0:
            low, up = edge + rows - 1, 4 * edge + rows - 1
        elif j == rows + 1:
            low, up = 2 * edge, 5 * edge
        else:
            low, up = j - 1, 3 * edge + j - 1
        source = jnp.where(
            scol < cols,
            jnp.where(scol == 0, cols + low, scol - 1),
            jnp.where(scol == 2 * cols - 1, cols + up, scol - cols + 1),
        )
        shifter[j] = (srow == source).astype(F32).astype(BF16)
    prow = lax.broadcasted_iota(jnp.int32, selector.shape, 0)
    pcol = lax.broadcasted_iota(jnp.int32, selector.shape, 1)
    wanted = jnp.where(prow < edge, prow * cols, (prow - edge) * cols + cols - 1)
    valid = (prow % edge) < rows
    selector[...] = ((pcol == wanted) & valid).astype(F32).astype(BF16)
    gap = cols // rows
    crow = lax.broadcasted_iota(jnp.int32, (cols, cols), 0)
    ccol = lax.broadcasted_iota(jnp.int32, (cols, cols), 1)
    for side in range(2):
        at = crow if side == 0 else (crow + 1) % cols
        for dr in range(3):
            j = at // gap + 2 - dr
            near = side * 3 * edge
            source = jnp.where(j == 0, near + edge + rows - 1, jnp.where(j == rows + 1, near + 2 * edge, near + j - 1))
            n = side * 3 + dr
            colsel[n * cols : (n + 1) * cols] = ((ccol == source) & (at % gap == 0)).astype(F32).astype(BF16)
    irow = lax.broadcasted_iota(jnp.int32, (width, width), 0)
    icol = lax.broadcasted_iota(jnp.int32, (width, width), 1)
    identity = (irow == icol).astype(F32).astype(BF16)

    loads[0].wait()
    loads[steps].wait()
    loads[steps + 1].wait()
    land = mask[...].astype(F32)[None]
    cells[0] = cell[...]
    gradc[...] = jnp.zeros_like(gradc)

    def place_z(step, first, count):
        for r in range(rows):
            tile = nat[pl.ds(r, count, stride=rows), :].astype(BF16)
            zwin[step, width + first : width + first + count, (r + 1) * cols : (r + 2) * cols] = tile

    def spread(ref, step=None):
        def put(b, carry):
            at = pl.ds(b * BLOCK, BLOCK)
            value = (ref[at] if step is None else ref[step, at]).astype(F32)
            nat[pl.ds(b * BLOCK * rows, BLOCK * rows), :] = value.reshape(BLOCK * rows, cols)
            return carry
        lax.fori_loop(0, ref.shape[-3] // BLOCK, put, 0)

    for step in range(steps):
        if step:
            loads[step].wait()

        def forward(b, carry):
            def gate(n):
                return pre[step, pl.ds(n * hidden + b * BLOCK, BLOCK)].astype(F32)
            at = pl.ds(b * BLOCK, BLOCK)
            gi, gf, go, gg = sigmoid(gate(0)), sigmoid(gate(1)), sigmoid(gate(2)), jnp.tanh(gate(3))
            new = gf * cells[step, at] + gi * gg
            tn = jnp.tanh(new)
            acts[step, 0, at] = gi
            acts[step, 1, at] = gf
            acts[step, 2, at] = go
            acts[step, 3, at] = gg
            cells[step + 1, at] = new
            tanhs[step, at] = tn
            nat[pl.ds(b * BLOCK * rows, BLOCK * rows), :] = (land * go * tn).reshape(BLOCK * rows, cols)
            return carry
        lax.fori_loop(0, hidden // BLOCK, forward, 0)
        if step + 1 < steps:
            place_z(step + 1, cin, hidden)

    loads[steps + 3].wait()

    def halo(step, d):
        dr, dc = SIDES[d]
        if dc == 0 and step == steps:
            first = cols if dr < 0 else rows * cols
            land_at = padded - cols if dr < 0 else 0
            src = zwin.at[:, pl.ds(width, width), pl.ds(first, cols)]
            dst = zwin.at[:, pl.ds(width, width), pl.ds(land_at, cols)]
        elif step == steps:
            src = zedges.at[1 if dc > 0 else 0]
            dst = zborder.at[pl.ds((d - 2) * edge, edge)]
        elif dc == 0:
            first = cols if dr < 0 else rows * cols
            land_at = padded - cols if dr < 0 else 0
            src = aall.at[step, pl.ds(gates, gates), pl.ds(first, cols)]
            dst = aall.at[step, pl.ds(gates, gates), pl.ds(land_at, cols)]
        else:
            src = edges.at[step, 1 if dc > 0 else 0]
            dst = border.at[step, pl.ds((d - 2) * edge, edge)]
        return pltpu.make_async_remote_copy(
            src_ref=src, dst_ref=dst, send_sem=send_sem.at[step, d], recv_sem=recv_sem.at[step, d],
            device_id=(row + dr, col + dc), device_id_type=MESH,
        )

    def start_halo(step):
        for d, (dr, dc) in enumerate(SIDES):
            @pl.when(inside(row + dr, col + dc))
            def _():
                halo(step, d).start()

    def wait_halo(step):
        for d, (dr, dc) in enumerate(SIDES):
            @pl.when(inside(row - dr, col - dc))
            def _():
                halo(step, d).wait_recv()

    def wait_sent(step):
        for d, (dr, dc) in enumerate(SIDES):
            @pl.when(inside(row + dr, col + dc))
            def _():
                halo(step, d).wait_send()

    def kernel_terms(step):
        own = aall[step, gates : 2 * gates, cols : padded - cols]
        for dr in range(3):
            at = slice(dr * 3 * width, (dr + 1) * 3 * width)
            term = nt(own, zwin[step, :, dr * cols : (dr + rows) * cols])
            kfull[:, at] = term if step == steps - 1 else kfull[:, at] + term

    def z_edges():
        for s in range(steps):
            picked = nt(selector[...], zwin[s, width : 2 * width, cols : padded - cols]).astype(BF16)
            zedges[0, :, s * width : (s + 1) * width] = picked[:edge]
            zedges[1, :, s * width : (s + 1) * width] = picked[edge:]

    def z_windows():
        sides = [nt(identity, zborder[:, s * width : (s + 1) * width]).astype(BF16) for s in range(steps)]
        for j in range(rows + 2):
            at = slice(j * cols, (j + 1) * cols)
            pairs = jnp.concatenate(
                [jnp.concatenate([zwin[s, width : 2 * width, at], sides[s]], axis=1) for s in range(steps)], axis=0
            )
            moved = nn(pairs, shifter[j]).astype(BF16)
            for s in range(steps):
                zwin[s, 0:width, at] = moved[s * width : (s + 1) * width, :cols]
                zwin[s, 2 * width : 3 * width, at] = moved[s * width : (s + 1) * width, cols:]

    def emit_inputs(step):
        def put(b, carry):
            at = pl.ds(b * BLOCK, BLOCK)
            gin_out[step, at] = nat[pl.ds((gates + b * BLOCK) * rows, BLOCK * rows), :].reshape(BLOCK, rows, cols).astype(BF16)
            return carry
        lax.fori_loop(0, cin // BLOCK, put, 0)
        store = pltpu.make_async_copy(gin_out.at[step], gin_hbm.at[step], store_sem.at[step])
        store.start()
        stores.append(store)

    def shift_row(step, j):
        at = slice(j * cols, (j + 1) * cols)
        moved = nn(aall[step, gates : 2 * gates, at], shifter[1, :cols]).astype(BF16)
        aall[step, 2 * gates : 3 * gates, at] = moved[:, :cols]
        aall[step, 0:gates, at] = moved[:, cols:]

    def transposed_own(step):
        for r in range(rows):
            shift_row(step, r + 1)
        product[...] = nn(weight_t[...], aall[step, :, cols : padded - cols])
        for r in range(rows):
            total = None
            for dr in range(3):
                if 0 <= r + 1 - dr < rows:
                    at = (r + 1 - dr) * cols
                    piece = product[dr * width : (dr + 1) * width, at : at + cols]
                    total = piece if total is None else total + piece
            ymain[:, r * cols : (r + 1) * cols] = total

    def transposed_halo(step):
        shift_row(step, 0)
        shift_row(step, rows + 1)
        above = nn(weight_t[2 * width : 3 * width], aall[step, :, 0:cols])
        below = nn(weight_t[0:width], aall[step, :, padded - cols : padded])
        picked = nn(colsel[...], border[step]).astype(BF16)
        sides = None
        for side in range(2):
            for dr in range(3):
                n, k = side * 3 + dr, 3 * dr + 2 - 2 * side
                piece = nn(picked[n * cols : (n + 1) * cols], weight[:, k * width : (k + 1) * width])
                sides = piece if sides is None else sides + piece
        sides = sides.T
        lane = lax.broadcasted_iota(jnp.int32, (width, cols), 1)
        outer = (lane == 0) | (lane == cols - 1)
        for r in range(rows):
            moved = pltpu.roll(sides, cols - gap * r, 1) if r else sides
            total = ymain[:, r * cols : (r + 1) * cols] + jnp.where(outer, moved, 0.0)
            if r == 0:
                total = total + above
            if r == rows - 1:
                total = total + below
            nat[pl.ds(gates * rows + r, cin, stride=rows), :] = total[:cin]
            nat[pl.ds((gates + cin) * rows + r, hidden, stride=rows), :] = total[cin:]

    bias = None
    stores = []
    for step in reversed(range(steps)):
        last = step == steps - 1

        def backward(b, carry):
            at = pl.ds(b * BLOCK, BLOCK)
            gi, gf, go, gg = (acts[step, n, at] for n in range(4))
            tn = tanhs[step, at]
            err = cot[step, at].astype(F32)
            if not last:
                err = err + nat[pl.ds((gates + cin + b * BLOCK) * rows, BLOCK * rows), :].reshape(BLOCK, rows, cols)
            err = land * err
            dc = gradc[at] + err * go * (1.0 - tn * tn)
            dci = dc * gi
            dcf = dc * gf
            parts = (
                dci * gg * (1.0 - gi),
                dcf * cells[step, at] * (1.0 - gf),
                err * tn * go * (1.0 - go),
                dci * (1.0 - gg * gg),
            )
            for n, value in enumerate(parts):
                nat[pl.ds((n * hidden + b * BLOCK) * rows, BLOCK * rows), :] = value.reshape(BLOCK * rows, cols)
            gradc[at] = dcf
            return carry
        lax.fori_loop(0, hidden // BLOCK, backward, 0)
        for r in range(rows):
            tile = nat[pl.ds(r, gates, stride=rows), :].astype(BF16)
            aall[step, gates : 2 * gates, (r + 1) * cols : (r + 2) * cols] = tile
            bias = tile.astype(F32) if last and r == 0 else bias + tile.astype(F32)
        own = aall[step, gates : 2 * gates, cols : padded - cols]
        picked = nt(selector[...], own).astype(BF16)
        edges[step, 0] = picked[:edge]
        edges[step, 1] = picked[edge:]
        if last:
            pl.semaphore_wait(barrier, number_of_partners(row, col, nrow, ncol, inside))
        start_halo(step)
        if last:
            loads[steps + 2].wait()
            for dr in range(3):
                for dc in range(3):
                    k = 3 * dr + dc
                    weight_t[dr * width : (dr + 1) * width, dc * gates : (dc + 1) * gates] = (
                        weight[:, k * width : (k + 1) * width].astype(F32).T.astype(BF16)
                    )
            transposed_own(step)
            loads[steps + 4].wait()
            loads[steps + 5].wait()
            spread(hid)
            place_z(0, cin, hidden)
            for s in range(steps):
                spread(inp, s)
                place_z(s, 0, cin)
            z_edges()
            start_halo(steps)
        elif step > 0:
            transposed_own(step)
            emit_inputs(step + 1)
            if step == steps - 2:
                wait_halo(steps)
                z_windows()
                kernel_terms(steps - 1)
            kernel_terms(step)
        else:
            kernel_terms(0)
        if step > 0:
            wait_halo(step)
            transposed_halo(step)

    lane = lax.broadcasted_iota(jnp.int32, (gates, lanes), 1)
    tail = lanes - 128

    def split(value):
        block = value[..., tail:]
        at = lax.broadcasted_iota(jnp.int32, block.shape, block.ndim - 1) + tail
        whole = jnp.where(at == part, block + pltpu.roll(block, 127, block.ndim - 1), block)
        own = jnp.where(at == part + 1, 0.0, whole)
        lost = pltpu.roll(own - own.astype(BF16).astype(F32), 1, block.ndim - 1)
        sent = jnp.where(at == part + 1, lost, own).astype(BF16)
        if not tail:
            return own, sent
        rest = value[..., :tail]
        return (
            jnp.concatenate([rest, own], axis=-1),
            jnp.concatenate([rest.astype(BF16), sent], axis=-1),
        )

    def first(c):
        return pltpu.make_async_remote_copy(
            src_ref=kbuf.at[1 - core, c], dst_ref=r1.at[c], send_sem=one_send.at[c], recv_sem=one_recv.at[c],
            device_id=(sibling, col), device_id_type=MESH,
        )

    def second(j, z):
        to = (col + j) % ncol
        return pltpu.make_async_remote_copy(
            src_ref=s1.at[to, z], dst_ref=r2.at[j - 1, z],
            send_sem=two_send.at[j - 1, z], recv_sem=two_recv.at[j - 1, z],
            device_id=(row, to), device_id_type=MESH,
        )

    bias = jnp.sum(bias, axis=1, keepdims=True) * scale
    for c in range(ncol):
        base, shift = part * c // 128 * 128, part * c % 128
        piece = kfull[:, base : base + lanes + 128]
        if shift:
            piece = pltpu.roll(piece, lanes + 128 - shift, 1)
        piece = jnp.where(lane < part, piece[:, :lanes] * scale, jnp.where(lane == part, bias, 0.0))
        sent = split(piece)[1]
        for r in range(nrow):
            kown[r % 2, c, r // 2] = piece[r * high : (r + 1) * high]
            kbuf[r % 2, c, r // 2] = sent[r * high : (r + 1) * high]
        first(c).start()

    def third(j):
        to = (zpos + j) % half
        return pltpu.make_async_remote_copy(
            src_ref=s2.at[to], dst_ref=r3.at[j - 1], send_sem=three_send.at[j], recv_sem=three_recv.at[j],
            device_id=(to * 2 + core, col), device_id_type=MESH,
        )

    transposed_own(0)
    order = [(zpos + j) % half for j in (*range(1, half), 0)]
    for j in (*range(1, ncol), 0):
        c = (col + j) % ncol
        first(c).wait_recv()
        for z in order:
            s1own[c, z], s1[c, z] = split(kown[core, c, z] + r1[c, z].astype(F32))
            if j:
                second(j, z).start()
    if steps > 1:
        emit_inputs(1)
    wait_halo(0)
    transposed_halo(0)
    emit_inputs(0)
    gh_out[...] = nat[pl.ds((gates + cin) * rows, hidden * rows), :].reshape(hidden, rows, cols)
    gc_out[...] = gradc[...]
    for n, (source, target) in enumerate(((gh_out, gh_hbm), (gc_out, gc_hbm))):
        store = pltpu.make_async_copy(source, target, store_sem.at[steps + n])
        store.start()
        stores.append(store)
    for n, z in enumerate(order):
        total = s1own[col, z]
        for j in range(1, ncol):
            second(j, z).wait_recv()
            total = total + r2[j - 1, z].astype(F32)
        s2own[z], s2[z] = split(total)
        if n + 1 < half:
            third(n + 1).start()
    total = s2own[zpos]
    for j in range(1, half):
        third(j).wait_recv()
        total = total + r3[j - 1].astype(F32)
    gk_out[...] = total[:, :part]
    block = total[:, tail:]
    line = lax.broadcasted_iota(jnp.int32, block.shape, 0)
    lane = lax.broadcasted_iota(jnp.int32, block.shape, 1)
    column = jnp.sum(jnp.where((lane == part - tail) | (lane == part + 1 - tail), block, 0.0), axis=1, keepdims=True)
    each = high // ncol
    wanted = line == lane + col * each
    bias_out[...] = jnp.sum(jnp.where(wanted, column, 0.0), axis=0, keepdims=True)[:, :each]
    for n, (source, target) in enumerate(((gk_out, gk_hbm), (bias_out, bias_hbm))):
        store = pltpu.make_async_copy(source, target, store_sem.at[steps + 2 + n])
        store.start()
        stores.append(store)
    for store in stores:
        store.wait()
    for step in range(steps + 1):
        wait_sent(step)
    for c in range(ncol):
        first(c).wait_send()
    for j in range(1, ncol):
        for z in range(half):
            second(j, z).wait_send()
    for j in range(1, half):
        third(j).wait_send()


def number_of_partners(row, col, nrow, ncol, inside):
    count = jnp.int32(1 + (ncol - 1) + (nrow // 2 - 1))
    for dr, dc in SIDES:
        count = count + inside(row + dr, col + dc).astype(jnp.int32)
    return count


def finish(*refs):
    sem = refs[-1]
    count = (len(refs) - 1) // 3
    sources, targets, held = refs[:count], refs[count : 2 * count], refs[2 * count : 3 * count]
    reads = [pltpu.make_async_copy(sources[n], held[n], sem.at[n]) for n in range(count)]
    writes = [pltpu.make_async_copy(held[n], targets[n], sem.at[count + n]) for n in range(count)]
    for copy in reads:
        copy.start()
    for n in range(count):
        reads[n].wait()
        writes[n].start()
    for copy in writes:
        copy.wait()


def shards(nrow, ncol, inputs, gate_pre, cotangent, hidden_init, cell_init, land_mask, kernel):
    steps, cin = inputs.shape[:2]
    hidden = hidden_init.shape[0]
    rows, cols = land_mask.shape
    width, gates = cin + hidden, 4 * hidden
    taps = kernel.shape[1]
    padded = (rows + 2) * cols
    edge = -(-rows // 16) * 16
    half, high, part = nrow // 2, gates // nrow, taps // ncol
    lanes = ((part + 1) // 128 + 1) * 128
    plane = (hidden, rows, cols)
    slots = max(half - 1, 1)
    scratch = [
        pltpu.VMEM(inputs.shape, BF16),
        pltpu.VMEM(gate_pre.shape, BF16),
        pltpu.VMEM(cotangent.shape, BF16),
        pltpu.VMEM(plane, BF16),
        pltpu.VMEM(plane, F32),
        pltpu.VMEM((rows, cols), jnp.int32),
        pltpu.VMEM(kernel.shape, BF16),
        pltpu.SemaphoreType.DMA((steps + 6,)),
        pltpu.VMEM((steps, 4) + plane, F32),
        pltpu.VMEM((steps + 1,) + plane, F32),
        pltpu.VMEM((steps,) + plane, F32),
        pltpu.VMEM(plane, F32),
        pltpu.VMEM(((gates + width) * rows, cols), F32),
        pltpu.VMEM((steps, 3 * width, padded), BF16),
        pltpu.VMEM((2, edge, steps * width), BF16),
        pltpu.VMEM((cols, steps * width), BF16),
        pltpu.VMEM((steps, 3 * gates, padded), BF16),
        pltpu.VMEM((steps, 2, edge, gates), BF16),
        pltpu.VMEM((steps, cols, gates), BF16),
        pltpu.VMEM((rows + 2, 2 * cols, 2 * cols), BF16),
        pltpu.VMEM((6 * cols, cols), BF16),
        pltpu.VMEM((3 * width, 3 * gates), BF16),
        pltpu.VMEM((2 * edge, rows * cols), BF16),
        pltpu.VMEM((3 * width, rows * cols), F32),
        pltpu.VMEM((width, rows * cols), F32),
        pltpu.VMEM((gates, taps + lanes + 128), F32),
        pltpu.VMEM((2, ncol, half, high, lanes), F32),
        pltpu.VMEM((2, ncol, half, high, lanes), BF16),
        pltpu.VMEM((ncol, half, high, lanes), BF16),
        pltpu.VMEM((ncol, half, high, lanes), F32),
        pltpu.VMEM((ncol, half, high, lanes), BF16),
        pltpu.VMEM((ncol - 1, half, high, lanes), BF16),
        pltpu.VMEM((half, high, lanes), F32),
        pltpu.VMEM((half, high, lanes), BF16),
        pltpu.VMEM((slots, high, lanes), BF16),
        pltpu.SemaphoreType.DMA((steps + 1, len(SIDES))),
        pltpu.SemaphoreType.DMA((steps + 1, len(SIDES))),
        pltpu.SemaphoreType.DMA((ncol,)),
        pltpu.SemaphoreType.DMA((ncol,)),
        pltpu.SemaphoreType.DMA((ncol - 1, half)),
        pltpu.SemaphoreType.DMA((ncol - 1, half)),
        pltpu.SemaphoreType.DMA((half,)),
        pltpu.SemaphoreType.DMA((half,)),
    ]
    each = high // ncol
    shapes = (
        jax.ShapeDtypeStruct(inputs.shape, BF16),
        jax.ShapeDtypeStruct(plane, F32),
        jax.ShapeDtypeStruct(plane, F32),
        jax.ShapeDtypeStruct((high, part), F32),
        jax.ShapeDtypeStruct((1, each), F32),
    )
    scratch += [pltpu.VMEM(shape.shape, shape.dtype) for shape in shapes]
    scratch.append(pltpu.SemaphoreType.DMA((steps + 4,)))
    hbm = pl.BlockSpec(memory_space=pltpu.HBM)
    results = pl.pallas_call(
        functools.partial(body, (steps, cin, hidden, rows, cols, nrow, ncol)),
        out_shape=shapes,
        in_specs=[hbm] * 7,
        out_specs=[hbm] * 5,
        scratch_shapes=scratch,
        compiler_params=pltpu.CompilerParams(
            collective_id=0, has_side_effects=True, vmem_limit_bytes=60 * 1024 * 1024
        ),
        name="convlstm_backward",
    )(inputs, gate_pre, cotangent, hidden_init, cell_init, land_mask, kernel)
    gin, gh, gc, gk, bias = pl.pallas_call(
        finish,
        out_shape=shapes,
        in_specs=[hbm] * 5,
        out_specs=[hbm] * 5,
        scratch_shapes=[pltpu.VMEM(shape.shape, shape.dtype) for shape in shapes] + [pltpu.SemaphoreType.DMA((10,))],
        compiler_params=pltpu.CompilerParams(vmem_limit_bytes=60 * 1024 * 1024),
        name="write_outputs",
    )(*results)
    return gin, gh, gc, gk, bias.reshape(each)


def solution(mesh):
    placed = (
        P(None, None, "row", "col"),
        P(None, None, "row", "col"),
        P(None, None, "row", "col"),
        P(None, "row", "col"),
        P(None, "row", "col"),
        P("row", "col"),
        P(),
    )
    return jax.shard_map(
        functools.partial(shards, mesh.shape["row"], mesh.shape["col"]),
        mesh=mesh,
        in_specs=placed,
        out_specs=(
            P(None, None, "row", "col"),
            P(None, "row", "col"),
            P(None, "row", "col"),
            P("row", "col"),
            P(("row", "col")),
        ),
        check_vma=False,
    )
```
